32 devices in a mesh: row: 8 (over z, x), col: 4 (over y, core).
Axes of the slice: x: 2, y: 2, z: 4, core: 2. Of those that a mesh axis runs over, the one named last changes fastest.
Arguments:
- attn: bfloat16 [2048, 16384], P('col', 'row'), may hold values from -6 to 6
- grad_out: bfloat16 [2048, 16384], P('row', 'col'), may hold values from -0.119628906 to 0.119628906
- weight: bfloat16 [16384, 16384], P('row', 'col'), may hold values from -2.09375 to 2.09375
- momentum: bfloat16 [16384, 16384], P('row', 'col'), may hold values from -3 to 3
Outputs:
- grad_in: bfloat16 [2048, 16384], P('col', 'row')
- new_weight: bfloat16 [16384, 16384], P('row', 'col')
- new_momentum: bfloat16 [16384, 16384], P('row', 'col')
The draws below stay inside these ranges and needn't reach their ends.
All inputs are finite; a program needn't handle non-finite values.
Results may differ from the reference program's by a relative error of at most 0.014.
Values may be sent and summed in bfloat16 or wider, within the bound.
No kernel may reach another device: no remote copies, remote signals or barrier semaphores. Data moves between devices by JAX's collectives and lax.ppermute only.
A program may use at most 192 MiB of HBM per device.

```python
import jax
import jax.numpy as jnp
from jax import lax

D = 16384
TOKENS = 2048
N_COL = 4


def strengthened(array, key, source, target, parts, factor):
    def block_of(dim):
        return (jnp.arange(array.shape[dim]) // (array.shape[dim] // parts)).reshape((-1,) + (1,) * (array.ndim - 1 - dim))

    near = jax.random.permutation(key, parts)[block_of(target)]
    far = (block_of(target) + parts // 2) % parts
    return jnp.where((block_of(source) == near) | (block_of(source) == far), factor * array, array)


def levels(key, shape, pieces, least, top_value):
    gain = 1.0
    for axis_at, blocks in pieces:
        draws = jax.random.uniform(jax.random.fold_in(jax.random.fold_in(key, 6), axis_at), (blocks,), jnp.float32, least / len(pieces), top_value / len(pieces))
        gain = gain * jnp.repeat(jnp.exp(draws), shape[axis_at] // blocks).reshape((-1,) + (1,) * (len(shape) - 1 - axis_at))
    return gain


def normal_values(stream_key, extent, scale, bound, pieces=(), kind=jnp.bfloat16):
    entries = jax.random.normal(stream_key, extent, jnp.float32) * scale
    if len(pieces) > 0:
        entries = levels(stream_key, extent, pieces, -0.22, 0.18) * entries
    return jnp.clip(entries, min=-bound, max=bound).astype(kind)


def heavy_noise(stream_key, dims, deviation, bound, cuts, heavy, held_as=jnp.bfloat16):
    drawn = deviation * jax.random.normal(stream_key, dims, jnp.float32)
    if cuts:
        drawn = drawn * levels(stream_key, dims, cuts, -0.22, 0.18)
    return jnp.clip(strengthened(drawn, jax.random.fold_in(stream_key, 3), *heavy), -bound, bound).astype(held_as)


def setup_inputs(seed: int = 0) -> dict:
    streams_of = jax.random.split(jax.random.key(seed), 5)
    return {
        "attn": normal_values(streams_of[0], (TOKENS, D), 1.0, 6.0, ((0, 4), (1, 8))),
        "grad_out": heavy_noise(streams_of[1], (TOKENS, D), 0.02, 0.119628906, ((0, 8), (1, 4)), (1, 0, 8, 2.0)),
        "weight": normal_values(streams_of[2], (D, D), 0.35, 2.09375, ((0, 8), (1, 4))),
        "momentum": normal_values(streams_of[3], (D, D), 0.5, 3.0, ((0, 8), (1, 4))),
    }


def reference(attn, grad_out, weight, momentum):
    block = D // N_COL
    weight_blocks = weight.reshape(D, N_COL, block).transpose(1, 0, 2)
    moment_blocks = momentum.reshape(D, N_COL, block).transpose(1, 0, 2)
    grad_blocks = grad_out.reshape(TOKENS, N_COL, block).transpose(1, 0, 2)

    def one_block(total, items):
        w_block, m_block, g_block = items
        grad_w = jnp.dot(attn.T, g_block, preferred_element_type=jnp.float32)
        partial_b = lax.dot_general(g_block, w_block, (((1,), (1,)), ((), ())), preferred_element_type=jnp.float32)
        partial_b = lax.optimization_barrier(partial_b.astype(jnp.bfloat16)).astype(jnp.float32)
        mom = 0.9 * m_block.astype(jnp.float32) + grad_w
        fresh_w = (w_block.astype(jnp.float32) - 0.25 * mom).astype(jnp.bfloat16)
        return total + partial_b, (fresh_w, mom.astype(jnp.bfloat16))

    start = jnp.zeros((TOKENS, D), jnp.float32)
    total, outs = lax.scan(one_block, start, (weight_blocks, moment_blocks, grad_blocks))
    new_weight = outs[0].transpose(1, 0, 2).reshape(D, D)
    new_momentum = outs[1].transpose(1, 0, 2).reshape(D, D)
    return total.astype(jnp.bfloat16), new_weight, new_momentum
```

```python
import functools

import jax
import jax.numpy as jnp
import numpy as np
from jax import lax
from jax.experimental import pallas as pl
from jax.experimental.pallas import tpu as pltpu
from jax.sharding import PartitionSpec as P

BF16 = jnp.bfloat16
F32 = jnp.float32
NT = (((1,), (1,)), ((), ()))
TN = (((0,), (0,)), ((), ()))
VMEM_BYTES = 60 << 20


def snake(n):
    return list(range(0, n, 2)) + list(range(n - 1 - (n % 2), 0, -2))


def tie(*xs):
    return lax.optimization_barrier(xs)


def fit(size, want):
    while size % want:
        want //= 2
    return want


def call(kernel, grid, in_specs, out_specs, out_shape, scalars=(), scratch=(), aliases=None, flops=0, bytes_accessed=0):
    return pl.pallas_call(
        kernel,
        grid_spec=pltpu.PrefetchScalarGridSpec(
            num_scalar_prefetch=len(scalars), grid=grid, in_specs=in_specs, out_specs=out_specs, scratch_shapes=scratch
        ),
        out_shape=out_shape,
        input_output_aliases=aliases or {},
        compiler_params=pltpu.CompilerParams(vmem_limit_bytes=VMEM_BYTES),
        cost_estimate=pl.CostEstimate(flops=flops, bytes_accessed=bytes_accessed, transcendentals=0),
    )


def tokens_of(refs, parts):
    halves = [refs[i : i + parts] for i in range(0, len(refs), parts)]
    rows = [h[0][...] if parts == 1 else jnp.concatenate([r[...] for r in h], axis=1) for h in halves]
    return jnp.concatenate(rows)


def grad_in_kernel(*refs, n, parts):
    total = lax.dot_general(tokens_of(refs[:n], parts), refs[n][...], NT, preferred_element_type=F32)
    refs[-1][...] = total.astype(BF16)


def grad_in_sorted_kernel(me, take, *refs, n, parts, n_out, half):
    total = lax.dot_general(tokens_of(refs[:n], parts), refs[n][...], NT, preferred_element_type=F32).astype(BF16)
    for s in range(n_out):
        upper = take[me[0] * n_out + s] > 0
        refs[n + 1 + s][...] = jnp.where(upper, total[half:], total[:half])


def grad_in_part(pieces, weight, take=None, me=None, tile=512):
    parts, half = len(pieces[0]), pieces[0][0].shape[0]
    feats, cols = weight.shape
    rows = half * len(pieces)
    tile = fit(feats, tile)
    flat = [x for p in pieces for x in p]
    specs = [pl.BlockSpec(x.shape, lambda i, *_: (0, 0)) for x in flat]
    specs.append(pl.BlockSpec((tile, cols), lambda i, *_: (i, 0)))
    cost = dict(flops=2 * rows * feats * cols, bytes_accessed=2 * (rows * cols + feats * cols + rows * feats))
    if take is None:
        kernel = functools.partial(grad_in_kernel, n=len(flat), parts=parts)
        out = pl.BlockSpec((rows, tile), lambda i: (0, i))
        return call(kernel, (feats // tile,), specs, out, jax.ShapeDtypeStruct((rows, feats), BF16), **cost)(*flat, weight)
    n_out = take.shape[1]
    kernel = functools.partial(grad_in_sorted_kernel, n=len(flat), parts=parts, n_out=n_out, half=half)
    outs = [pl.BlockSpec((half, tile), lambda i, *_: (0, i))] * n_out
    shapes = [jax.ShapeDtypeStruct((half, feats), BF16)] * n_out
    return call(kernel, (feats // tile,), specs, outs, shapes, scalars=(me, take), **cost)(
        me, jnp.asarray(take.reshape(-1), jnp.int32), *flat, weight
    )


def assemble(dst, refs):
    at = 0
    for r in refs:
        dst[at : at + r.shape[0], :] = r[...]
        at += r.shape[0]


def pass_kernel(_, __, *refs, n, n_grads, last, n_old, rows):
    attn, grads, rest = refs[:n], refs[n : n + n_grads], refs[n + n_grads :]
    if last:
        acc_ref, w_ref = rest[:2]
        new_w, new_m, attn_s, grad_s = rest[2 + n_old :]
    else:
        m_ref, out, attn_s, grad_s = rest

    @pl.when(pl.program_id(0) == 0)
    def _():
        assemble(attn_s, attn)

    assemble(grad_s, grads)
    for c in range(0, attn_s.shape[1], rows):
        here = slice(c, c + rows)
        add = lax.dot_general(attn_s[:, here], grad_s[...], TN, preferred_element_type=F32)
        if last:
            mom = acc_ref[here].astype(F32) + add
            new_w[here] = (w_ref[here].astype(F32) - 0.25 * mom).astype(BF16)
            new_m[here] = mom.astype(BF16)
        else:
            out[here] = (0.9 * m_ref[here].astype(F32) + add).astype(out.dtype)


def token_pass(me, order, attn_all, pieces, wides, first_col=0, n_cols=None, old=(), out_dtype=None, tile=512):
    last = len(wides) == 2
    n = len(pieces)
    half = pieces[0][0].shape[0]
    feats, cols = wides[0].shape
    n_cols = n_cols or cols
    tile = fit(n_cols, tile)
    base = first_col // tile
    specs = [pl.BlockSpec((half, feats), lambda j, me, o, i=i: (o[me[0] * n + i], 0)) for i in range(n)]
    specs += [pl.BlockSpec((half, tile), lambda j, *_, c=(first_col - at) // tile: (0, j + c)) for _, at in pieces]
    wide = pl.BlockSpec((feats, tile), lambda j, *_: (0, j + base))
    specs += [wide] * len(wides) + [pl.BlockSpec(memory_space=pl.ANY)] * len(old)
    shape = jax.ShapeDtypeStruct((feats, cols), BF16 if last else out_dtype)
    return call(
        functools.partial(pass_kernel, n=n, n_grads=n, last=last, n_old=len(old), rows=fit(feats, 512)),
        (n_cols // tile,),
        specs,
        [wide, wide] if last else wide,
        [shape, shape] if last else shape,
        scalars=(me, order),
        scratch=[pltpu.VMEM((n * half, feats), BF16), pltpu.VMEM((n * half, tile), BF16)],
        aliases={2 + 2 * n + 2 + i: i for i in range(len(old))},
        flops=2 * n * half * feats * n_cols,
        bytes_accessed=8 * feats * n_cols,
    )(me, jnp.asarray(order.reshape(-1), jnp.int32), *([attn_all] * n), *[x for x, _ in pieces], *wides, *old)


def pair_sum_kernel(_, __, mine, other, out):
    out[...] = (mine[...].astype(F32) + other[...].astype(F32)).astype(BF16)


def pair_sum(me, which, mine, other, half):
    n, width = which.shape[1], mine.shape[1]
    picked = pl.BlockSpec((half, width), lambda i, me, w: (w[me[0] * n + i], 0))
    return call(
        pair_sum_kernel,
        (n,),
        [picked, picked],
        pl.BlockSpec((half, width), lambda i, *_: (i, 0)),
        jax.ShapeDtypeStruct((n * half, width), BF16),
        scalars=(me, which),
        bytes_accessed=6 * n * half * width,
    )(me, jnp.asarray(which.reshape(-1), jnp.int32), mine, other)


def place_kernel(me, _, valid, __, *refs, spans, total_slots):
    out, i = refs[-1], pl.program_id(0)
    flag = valid[me[0] * total_slots + i]
    at = 0
    for first, slots, n in spans:
        mine = refs[at : at + n]
        at += n

        @pl.when((flag == 1) & (i >= first) & (i < first + slots))
        def _():
            total = mine[0][...].astype(F32)
            for r in mine[1:]:
                total = total + r[...].astype(F32)
            out[...] = total.astype(BF16)

    if len(refs) > at + 1:

        @pl.when(flag == 2)
        def _():
            out[...] = refs[at][...]


def place(me, groups, out, shape, half):
    which = np.concatenate([g[0][0] for g in groups], axis=1)
    valid = np.concatenate([g[0][1] for g in groups], axis=1)
    where = np.concatenate([g[0][2] for g in groups], axis=1)
    n = which.shape[1]
    for d in range(len(valid)):
        real = np.flatnonzero(valid[d])
        if len(real) == 0:
            valid[d], where[d] = 2, 0
            continue
        for s in range(n):
            before = real[real <= s]
            where[d, s] = where[d, before[-1] if len(before) else real[0]]
    width = shape[1]
    specs, args, spans, first = [], [], [], 0
    for tables, picked, received in groups:
        slots = tables[0].shape[1]
        at = lambda i, f=first, s=slots: jnp.clip(i, f, f + s - 1)
        specs += [pl.BlockSpec((half, width), lambda i, me, w, v, p, at=at: (w[me[0] * n + at(i)], 0)) for _ in picked]
        specs += [pl.BlockSpec((half, width), lambda i, me, w, v, p, at=at, f=first: (at(i) - f, 0)) for _ in received]
        args += [*picked, *received]
        spans.append((first, slots, len(picked) + len(received)))
        first += slots
    spec = pl.BlockSpec((half, width), lambda i, me, w, v, p: (p[me[0] * n + i], 0))
    aliases = {}
    if out is not None:
        specs.append(spec if (valid == 2).any() else pl.BlockSpec(memory_space=pl.ANY))
        args.append(out)
        aliases = {4 + len(args) - 1: 0}
    kernel = functools.partial(place_kernel, spans=spans, total_slots=n)
    if out is not None and not (valid == 2).any():
        inner = kernel
        kernel = lambda *refs: inner(*refs[:-2], refs[-1])
    return call(
        kernel,
        (n,),
        specs,
        spec,
        jax.ShapeDtypeStruct(shape, BF16),
        scalars=(me, which, valid, where),
        aliases=aliases,
        bytes_accessed=8 * n * half * width,
    )(me, *[jnp.asarray(t.reshape(-1), jnp.int32) for t in (which, valid, where)], *args)


def body(n_row, n_col, attn, grad_out, weight, momentum):
    ring = np.array(snake(n_row))
    pos = np.argsort(ring)
    right = [(int(ring[i]), int(ring[(i + 1) % n_row])) for i in range(n_row)]
    left = [(b, a) for a, b in right]
    block, cols = grad_out.shape
    half = block // 2
    per_owner = n_row // n_col
    n_y = n_col // 2
    devices = [(r, c) for r in range(n_row) for c in range(n_col)]
    me = (lax.axis_index("row") * n_col + lax.axis_index("col")).astype(jnp.int32).reshape(1)
    out_shape = (per_owner * block, weight.shape[0])

    arrives = np.zeros((n_row, n_row, 2), np.int32)
    for r in range(n_row):
        for k in range(n_row):
            arrives[r, k, 0] = 2 * ring[(pos[r] - k) % n_row]
            arrives[r, k, 1] = 2 * ring[(pos[r] + k) % n_row] + 1

    def order_of(steps):
        return np.stack([arrives[r, np.array(steps)].reshape(-1) for r, _ in devices])

    def tables_of(steps):
        halves = arrives[:, np.array(steps), :].reshape(n_row, -1)
        owner = halves // (2 * per_owner)
        slots = max(int(np.sum(owner[r] == c)) for r, c in devices)
        which, valid, where = (np.zeros((n_row * n_col, slots), np.int32) for _ in range(3))
        for d, (r, c) in enumerate(devices):
            own = np.flatnonzero(owner[r] == c)
            spots = list(halves[r, own] % (2 * per_owner))
            spots += [s for s in range(2 * per_owner) if s not in spots]
            which[d, : len(own)] = own
            valid[d, : len(own)] = 1
            where[d] = spots[:slots]
        return which, valid, where

    def route(valid, shift):
        to = [(r, (c + shift) % n_col) for r, c in devices]
        return [(d, r * n_col + c) for d, (r, c) in enumerate(to) if valid[r * n_col + c].any()]

    def shifted(table, shift):
        return np.stack([table[r * n_col + (c + shift) % n_col] for r, c in devices])

    def reduce_in_pairs(steps, part):
        tables = tables_of(steps)
        (other,) = yield [lax.ppermute(part, "col", [(c, c ^ 1) for c in range(n_col)])]
        received = []
        for s in range(2, n_col, 2):
            sent = pair_sum(me, shifted(tables[0], s), part, other, half)
            received.append(lax.ppermute(sent, ("row", "col"), route(tables[1], s)))
        received = yield received
        done.append((tables, [part, other], received))

    def reduce_direct(step, parts):
        tables = tables_of([step])
        received = yield [lax.ppermute(parts[s], ("row", "col"), route(tables[1], s)) for s in range(1, n_col)]
        done.append((tables, [], [parts[0], *received]))

    def sorted_part(step):
        which = tables_of([step])[0]
        take = np.concatenate([shifted(which, s) for s in range(n_col)], axis=1)
        return grad_in_part(pieces_of([step]), weight, take, me)

    attn_all = lax.all_gather(attn, "col", axis=0, tiled=True)
    arrived = {0: (grad_out[:half], grad_out[half:])}
    pieces_of = lambda steps: [(x,) for k in steps for x in arrived[k]]
    whole_pieces = lambda steps: [(x, 0) for k in steps for x in arrived[k]]

    top = n_row - 1
    mid = n_row // 2
    early = list(range(0, mid - 1))
    late = list(range(mid - 1, n_row))
    at_work = {
        2: [("pairs", [0, 1])],
        mid: [("pairs", list(range(2, mid)))],
        mid + 1: [("first",)],
        top - 1: [("pairs", list(range(mid, top - 1)))],
        top: [("direct", top - 1)],
    }
    done, moving = [], []
    grad_in = None
    acc = None

    def turn(on_link, work):
        nonlocal moving
        flights = [f for _, f in moving]
        on_link, work, flights = tie(on_link, work, flights)
        moving = [[g, f] for (g, _), f in zip(moving, flights)]
        return on_link, work

    def advance():
        nonlocal moving
        still = []
        for g, f in moving:
            try:
                still.append([g, g.send(f)])
            except StopIteration:
                pass
        moving = still

    for k in range(1, n_row):
        a, b = arrived[k - 1]
        nxt = (lax.ppermute(a, "row", right), lax.ppermute(b, "row", left))
        jobs = at_work.get(k, [])
        results = []
        for job in jobs:
            if job[0] == "pairs":
                results.append([grad_in_part(pieces_of(job[1]), weight)])
            elif job[0] == "direct":
                results.append(sorted_part(job[1]))
            else:
                results.append([token_pass(me, order_of(early), attn_all, whole_pieces(early), (momentum,), out_dtype=BF16)])
        arrived[k], results = turn(nxt, results)
        advance()
        for job, result in zip(jobs, results):
            if job[0] == "first":
                acc = result[0]
                continue
            g = reduce_in_pairs(job[1], result[0]) if job[0] == "pairs" else reduce_direct(job[1], result)
            moving.append([g, next(g)])
    parts = sorted_part(top)
    if done:
        grad_in = place(me, done, None, out_shape, half)
        done.clear()
    parts, acc = tie(parts, acc)
    g = reduce_direct(top, parts)
    moving.append([g, next(g)])
    new_w, new_m = token_pass(me, order_of(late), attn_all, whole_pieces(late), (acc, weight))
    _, (new_w, new_m) = turn((), (new_w, new_m))
    while moving:
        advance()
    grad_in = place(me, done, grad_in, out_shape, half)
    return grad_in, new_w, new_m


def solution(mesh):
    n_row, n_col = mesh.shape["row"], mesh.shape["col"]
    spec, act = P("row", "col"), P("col", "row")

    def shards(attn, grad_out, weight, momentum):
        return body(n_row, n_col, attn, grad_out, weight, momentum)

    return jax.shard_map(shards, mesh=mesh, in_specs=(act, spec, spec, spec), out_specs=(act, spec, spec), check_vma=False)
```

```python
import functools

import jax
import jax.numpy as jnp
import numpy as np
from jax import lax
from jax.experimental import pallas as pl
from jax.experimental.pallas import tpu as pltpu
from jax.sharding import PartitionSpec as P

BF16 = jnp.bfloat16
F32 = jnp.float32
NT = (((1,), (1,)), ((), ()))
TN = (((0,), (0,)), ((), ()))
VMEM_BYTES = 60 << 20


def snake(n):
    return list(range(0, n, 2)) + list(range(n - 1 - (n % 2), 0, -2))


def tie(*xs):
    return lax.optimization_barrier(xs)


def fit(size, want):
    while size % want:
        want //= 2
    return want


def call(kernel, grid, in_specs, out_specs, out_shape, scalars=(), scratch=(), aliases=None, flops=0, bytes_accessed=0):
    return pl.pallas_call(
        kernel,
        grid_spec=pltpu.PrefetchScalarGridSpec(
            num_scalar_prefetch=len(scalars), grid=grid, in_specs=in_specs, out_specs=out_specs, scratch_shapes=scratch
        ),
        out_shape=out_shape,
        input_output_aliases=aliases or {},
        compiler_params=pltpu.CompilerParams(vmem_limit_bytes=VMEM_BYTES),
        cost_estimate=pl.CostEstimate(flops=flops, bytes_accessed=bytes_accessed, transcendentals=0),
    )


def tokens_of(refs, parts):
    halves = [refs[i : i + parts] for i in range(0, len(refs), parts)]
    rows = [h[0][...] if parts == 1 else jnp.concatenate([r[...] for r in h], axis=1) for h in halves]
    return jnp.concatenate(rows)


def grad_in_kernel(*refs, n, parts):
    total = lax.dot_general(tokens_of(refs[:n], parts), refs[n][...], NT, preferred_element_type=F32)
    refs[-1][...] = total.astype(BF16)


def grad_in_sorted_kernel(me, take, *refs, n, parts, n_out, half):
    total = lax.dot_general(tokens_of(refs[:n], parts), refs[n][...], NT, preferred_element_type=F32).astype(BF16)
    for s in range(n_out):
        upper = take[me[0] * n_out + s] > 0
        refs[n + 1 + s][...] = jnp.where(upper, total[half:], total[:half])


def grad_in_part(pieces, weight, take=None, me=None, tile=512):
    parts, half = len(pieces[0]), pieces[0][0].shape[0]
    feats, cols = weight.shape
    rows = half * len(pieces)
    tile = fit(feats, tile)
    flat = [x for p in pieces for x in p]
    specs = [pl.BlockSpec(x.shape, lambda i, *_: (0, 0)) for x in flat]
    specs.append(pl.BlockSpec((tile, cols), lambda i, *_: (i, 0)))
    cost = dict(flops=2 * rows * feats * cols, bytes_accessed=2 * (rows * cols + feats * cols + rows * feats))
    if take is None:
        kernel = functools.partial(grad_in_kernel, n=len(flat), parts=parts)
        out = pl.BlockSpec((rows, tile), lambda i: (0, i))
        return call(kernel, (feats // tile,), specs, out, jax.ShapeDtypeStruct((rows, feats), BF16), **cost)(*flat, weight)
    n_out = take.shape[1]
    kernel = functools.partial(grad_in_sorted_kernel, n=len(flat), parts=parts, n_out=n_out, half=half)
    outs = [pl.BlockSpec((half, tile), lambda i, *_: (0, i))] * n_out
    shapes = [jax.ShapeDtypeStruct((half, feats), BF16)] * n_out
    return call(kernel, (feats // tile,), specs, outs, shapes, scalars=(me, take), **cost)(
        me, jnp.asarray(take.reshape(-1), jnp.int32), *flat, weight
    )


def assemble(dst, refs):
    at = 0
    for r in refs:
        dst[at : at + r.shape[0], :] = r[...]
        at += r.shape[0]


def pass_kernel(_, __, *refs, n, n_grads, last, n_old, rows):
    attn, grads, rest = refs[:n], refs[n : n + n_grads], refs[n + n_grads :]
    if last:
        acc_ref, w_ref = rest[:2]
        new_w, new_m, attn_s, grad_s = rest[2 + n_old :]
    else:
        m_ref, out, attn_s, grad_s = rest

    @pl.when(pl.program_id(0) == 0)
    def _():
        assemble(attn_s, attn)

    assemble(grad_s, grads)
    for c in range(0, attn_s.shape[1], rows):
        here = slice(c, c + rows)
        add = lax.dot_general(attn_s[:, here], grad_s[...], TN, preferred_element_type=F32)
        if last:
            mom = acc_ref[here].astype(F32) + add
            new_w[here] = (w_ref[here].astype(F32) - 0.25 * mom).astype(BF16)
            new_m[here] = mom.astype(BF16)
        else:
            out[here] = (0.9 * m_ref[here].astype(F32) + add).astype(out.dtype)


def token_pass(me, order, attn_all, pieces, wides, first_col=0, n_cols=None, old=(), out_dtype=None, tile=512):
    last = len(wides) == 2
    n = len(pieces)
    half = pieces[0][0].shape[0]
    feats, cols = wides[0].shape
    n_cols = n_cols or cols
    tile = fit(n_cols, tile)
    base = first_col // tile
    specs = [pl.BlockSpec((half, feats), lambda j, me, o, i=i: (o[me[0] * n + i], 0)) for i in range(n)]
    specs += [pl.BlockSpec((half, tile), lambda j, *_, c=(first_col - at) // tile: (0, j + c)) for _, at in pieces]
    wide = pl.BlockSpec((feats, tile), lambda j, *_: (0, j + base))
    specs += [wide] * len(wides) + [pl.BlockSpec(memory_space=pl.ANY)] * len(old)
    shape = jax.ShapeDtypeStruct((feats, cols), BF16 if last else out_dtype)
    return call(
        functools.partial(pass_kernel, n=n, n_grads=n, last=last, n_old=len(old), rows=fit(feats, 512)),
        (n_cols // tile,),
        specs,
        [wide, wide] if last else wide,
        [shape, shape] if last else shape,
        scalars=(me, order),
        scratch=[pltpu.VMEM((n * half, feats), BF16), pltpu.VMEM((n * half, tile), BF16)],
        aliases={2 + 2 * n + 2 + i: i for i in range(len(old))},
        flops=2 * n * half * feats * n_cols,
        bytes_accessed=8 * feats * n_cols,
    )(me, jnp.asarray(order.reshape(-1), jnp.int32), *([attn_all] * n), *[x for x, _ in pieces], *wides, *old)


def pair_sum_kernel(_, __, *refs, n):
    ins, outs = refs[: 2 * n], refs[2 * n :]
    for s in range(n):
        outs[s][...] = (ins[2 * s][...].astype(F32) + ins[2 * s + 1][...].astype(F32)).astype(BF16)


def pair_sum(me, which, mine, other, half, tile=512):
    n, width = which.shape[1], mine.shape[1]
    tile = fit(width, tile)
    picked = [pl.BlockSpec((half, tile), lambda i, me, w, s=s: (w[me[0] * n + s], i)) for s in range(n) for _ in range(2)]
    return call(
        functools.partial(pair_sum_kernel, n=n),
        (width // tile,),
        picked,
        [pl.BlockSpec((half, tile), lambda i, *_: (0, i))] * n,
        [jax.ShapeDtypeStruct((half, width), BF16)] * n,
        scalars=(me, which),
        bytes_accessed=6 * n * half * width,
    )(me, jnp.asarray(which.reshape(-1), jnp.int32), *([mine, other] * n))


def place_kernel(me, _, valid, __, *refs, spans, total_slots):
    out, i = refs[-1], pl.program_id(0)
    flag = valid[me[0] * total_slots + i]
    at = 0
    for counts, n_picked in spans:
        picked = refs[at : at + n_picked]
        at += n_picked
        for slot, n_received in counts:
            mine = [*picked, *refs[at : at + n_received]]
            at += n_received

            @pl.when((flag == 1) & (i == slot))
            def _():
                total = mine[0][...].astype(F32)
                for r in mine[1:]:
                    total = total + r[...].astype(F32)
                out[...] = total.astype(BF16)

    if len(refs) > at + 1:

        @pl.when(flag == 2)
        def _():
            out[...] = refs[at][...]


def place(me, groups, out, shape, half):
    which = np.concatenate([g[0][0] for g in groups], axis=1)
    valid = np.concatenate([g[0][1] for g in groups], axis=1)
    where = np.concatenate([g[0][2] for g in groups], axis=1)
    n = which.shape[1]
    for d in range(len(valid)):
        real = np.flatnonzero(valid[d])
        if len(real) == 0:
            valid[d], where[d] = 2, 0
            continue
        for s in range(n):
            before = real[real <= s]
            where[d, s] = where[d, before[-1] if len(before) else real[0]]
    width = shape[1]
    specs, args, spans, first = [], [], [], 0
    for tables, picked, received in groups:
        slots = tables[0].shape[1]
        at = lambda i, f=first, s=slots: jnp.clip(i, f, f + s - 1)
        specs += [pl.BlockSpec((half, width), lambda i, me, w, v, p, at=at: (w[me[0] * n + at(i)], 0)) for _ in picked]
        args += picked
        for r in received:
            specs += [pl.BlockSpec((half, width), lambda i, *_: (0, 0)) for _ in r]
            args += r
        spans.append(([(first + s, len(r)) for s, r in enumerate(received)], len(picked)))
        first += slots
    spec = pl.BlockSpec((half, width), lambda i, me, w, v, p: (p[me[0] * n + i], 0))
    aliases = {}
    kernel = functools.partial(place_kernel, spans=spans, total_slots=n)
    if out is not None:
        keep = (valid == 2).any()
        specs.append(spec if keep else pl.BlockSpec(memory_space=pl.ANY))
        args.append(out)
        aliases = {4 + len(args) - 1: 0}
        if not keep:
            inner = kernel
            kernel = lambda *refs: inner(*refs[:-2], refs[-1])
    return call(
        kernel,
        (n,),
        specs,
        spec,
        jax.ShapeDtypeStruct(shape, BF16),
        scalars=(me, which, valid, where),
        aliases=aliases,
        bytes_accessed=8 * n * half * width,
    )(me, *[jnp.asarray(t.reshape(-1), jnp.int32) for t in (which, valid, where)], *args)


def body(n_row, n_col, attn, grad_out, weight, momentum):
    ring = np.array(snake(n_row))
    pos = np.argsort(ring)
    right = [(int(ring[i]), int(ring[(i + 1) % n_row])) for i in range(n_row)]
    left = [(b, a) for a, b in right]
    block, cols = grad_out.shape
    half = block // 2
    per_owner = n_row // n_col
    n_y = n_col // 2
    devices = [(r, c) for r in range(n_row) for c in range(n_col)]
    me = (lax.axis_index("row") * n_col + lax.axis_index("col")).astype(jnp.int32).reshape(1)
    out_shape = (per_owner * block, weight.shape[0])

    arrives = np.zeros((n_row, n_row, 2), np.int32)
    for r in range(n_row):
        for k in range(n_row):
            arrives[r, k, 0] = 2 * ring[(pos[r] - k) % n_row]
            arrives[r, k, 1] = 2 * ring[(pos[r] + k) % n_row] + 1

    def order_of(steps):
        return np.stack([arrives[r, np.array(steps)].reshape(-1) for r, _ in devices])

    def tables_of(steps):
        halves = arrives[:, np.array(steps), :].reshape(n_row, -1)
        owner = halves // (2 * per_owner)
        slots = max(int(np.sum(owner[r] == c)) for r, c in devices)
        which, valid, where = (np.zeros((n_row * n_col, slots), np.int32) for _ in range(3))
        for d, (r, c) in enumerate(devices):
            own = np.flatnonzero(owner[r] == c)
            spots = list(halves[r, own] % (2 * per_owner))
            spots += [s for s in range(2 * per_owner) if s not in spots]
            which[d, : len(own)] = own
            valid[d, : len(own)] = 1
            where[d] = spots[:slots]
        return which, valid, where

    def route(valid, shift, slot):
        to = [(r, (c + shift) % n_col) for r, c in devices]
        return [(d, r * n_col + c) for d, (r, c) in enumerate(to) if valid[r * n_col + c, slot]]

    def send(arrays, valid, shift):
        return [lax.ppermute(x, ("row", "col"), route(valid, shift, s)) for s, x in enumerate(arrays)]

    def shifted(table, shift):
        return np.stack([table[r * n_col + (c + shift) % n_col] for r, c in devices])

    def reduce_in_pairs(steps, part, late=False):
        tables = tables_of(steps)
        other = lax.ppermute(part, "col", [(c, c ^ 1) for c in range(n_col)])
        shifts = range(2, n_col, 2)
        sums = [pair_sum(me, shifted(tables[0], s), part, other, half) for s in shifts]
        other, sums = yield other, sums
        received = [send(sums[i], tables[1], s) for i, s in enumerate(shifts)]
        if late:
            yield ()
        received = yield received
        done.append((tables, [part, other], [list(r) for r in zip(*received)]))

    def reduce_direct(step, parts):
        tables = tables_of([step])
        received = yield [send([parts[s]], tables[1], s)[0] for s in range(1, n_col)]
        done.append((tables, [], [[parts[0], *received]]))

    def sorted_part(step):
        which = tables_of([step])[0]
        take = np.concatenate([shifted(which, s) for s in range(n_col)], axis=1)
        return grad_in_part(pieces_of([step]), weight, take, me)

    attn_all = lax.all_gather(attn, "col", axis=0, tiled=True)
    arrived = {0: (grad_out[:half], grad_out[half:])}
    pieces_of = lambda steps: [(x,) for k in steps for x in arrived[k]]
    whole_pieces = lambda steps: [(x, 0) for k in steps for x in arrived[k]]

    top = n_row - 1
    mid = n_row // 2
    early = list(range(0, mid - 1))
    late = list(range(mid - 1, n_row))
    at_work = {
        2: ["pairs", [0, 1]],
        mid: ["first"],
        mid + 1: ["pairs", list(range(2, mid))],
        top - 1: ["pairs", list(range(mid, top - 1))],
        top: ["pairs", [top - 1]],
    }
    done, moving = [], []
    grad_in = None
    acc = None

    def turn(on_link, work):
        nonlocal moving
        on_link, work, flights = tie(on_link, work, [f for _, f in moving])
        moving = [[g, f] for (g, _), f in zip(moving, flights)]
        return on_link, work

    def advance():
        nonlocal moving
        still = []
        for g, f in moving:
            try:
                still.append([g, g.send(f)])
            except StopIteration:
                pass
        moving = still

    def begin(g):
        moving.append([g, next(g)])

    for k in range(1, n_row):
        a, b = arrived[k - 1]
        nxt = (lax.ppermute(a, "row", right), lax.ppermute(b, "row", left))
        job = at_work.get(k, ["none"])
        work = ()
        if job[0] == "pairs":
            work = grad_in_part(pieces_of(job[1]), weight)
        elif job[0] == "first":
            work = token_pass(me, order_of(early), attn_all, whole_pieces(early), (momentum,), out_dtype=BF16)
        if k == top:
            grad_in = place(me, done, None, out_shape, half) if done else jnp.zeros(out_shape, BF16)
            done.clear()
            work = (work, grad_in)
        arrived[k], work = turn(nxt, work)
        if k == top:
            work, grad_in = work
        advance()
        if job[0] == "pairs":
            begin(reduce_in_pairs(job[1], work, late=k == 2))
        elif job[0] == "first":
            acc = work
    parts = sorted_part(top)
    sums = [f for g, f in moving if len(f) == 2 and not isinstance(f, list)]
    parts, acc, sums = tie(parts, acc, sums)
    sums = iter(sums)
    moving = [[g, next(sums) if len(f) == 2 and not isinstance(f, list) else f] for g, f in moving]
    still = []
    for g, f in moving:
        still.append([g, g.send(f)] if not isinstance(f, list) else [g, f])
    moving = still
    begin(reduce_direct(top, parts))
    new_w, new_m = token_pass(me, order_of(late), attn_all, whole_pieces(late), (acc, weight))
    _, (new_w, new_m) = turn((), (new_w, new_m))
    while moving:
        advance()
    grad_in = place(me, done, grad_in, out_shape, half)
    return grad_in, new_w, new_m


def solution(mesh):
    n_row, n_col = mesh.shape["row"], mesh.shape["col"]
    spec, act = P("row", "col"), P("col", "row")

    def shards(attn, grad_out, weight, momentum):
        return body(n_row, n_col, attn, grad_out, weight, momentum)

    return jax.shard_map(shards, mesh=mesh, in_specs=(act, spec, spec, spec), out_specs=(act, spec, spec), check_vma=False)
```

```python
import functools

import jax
import jax.numpy as jnp
import numpy as np
from jax import lax
from jax.experimental import pallas as pl
from jax.experimental.pallas import tpu as pltpu
from jax.sharding import PartitionSpec as P

BF16 = jnp.bfloat16
F32 = jnp.float32
NT = (((1,), (1,)), ((), ()))
TN = (((0,), (0,)), ((), ()))
VMEM_BYTES = 60 << 20
GRAD_IN_VMEM, SUM_VMEM = 50 << 20, 24 << 20


def snake(n):
    return list(range(0, n, 2)) + list(range(n - 1 - (n % 2), 0, -2))


def tie(*xs):
    return lax.optimization_barrier(xs)


def fit(size, want):
    while size % want:
        want //= 2
    return want


def call(kernel, grid, in_specs, out_specs, out_shape, scalars=(), scratch=(), aliases=None, flops=0, bytes_accessed=0, vmem=VMEM_BYTES):
    return pl.pallas_call(
        kernel,
        grid_spec=pltpu.PrefetchScalarGridSpec(
            num_scalar_prefetch=len(scalars), grid=grid, in_specs=in_specs, out_specs=out_specs, scratch_shapes=scratch
        ),
        out_shape=out_shape,
        input_output_aliases=aliases or {},
        compiler_params=pltpu.CompilerParams(vmem_limit_bytes=vmem),
        cost_estimate=pl.CostEstimate(flops=flops, bytes_accessed=bytes_accessed, transcendentals=0),
    )


def tokens_of(refs, parts):
    halves = [refs[i : i + parts] for i in range(0, len(refs), parts)]
    rows = [h[0][...] if parts == 1 else jnp.concatenate([r[...] for r in h], axis=1) for h in halves]
    return jnp.concatenate(rows)


def grad_in_kernel(*refs, n, parts):
    total = lax.dot_general(tokens_of(refs[:n], parts), refs[n][...], NT, preferred_element_type=F32)
    refs[-1][...] = total.astype(BF16)


def grad_in_sorted_kernel(me, take, *refs, n, parts, n_out, half):
    total = lax.dot_general(tokens_of(refs[:n], parts), refs[n][...], NT, preferred_element_type=F32).astype(BF16)
    for s in range(n_out):
        upper = take[me[0] * n_out + s] > 0
        refs[n + 1 + s][...] = jnp.where(upper, total[half:], total[:half])


def grad_in_part(pieces, weight, take=None, me=None, tile=512):
    parts, half = len(pieces[0]), pieces[0][0].shape[0]
    feats, cols = weight.shape
    rows = half * len(pieces)
    tile = fit(feats, tile)
    flat = [x for p in pieces for x in p]
    specs = [pl.BlockSpec(x.shape, lambda i, *_: (0, 0)) for x in flat]
    specs.append(pl.BlockSpec((tile, cols), lambda i, *_: (i, 0)))
    cost = dict(vmem=GRAD_IN_VMEM, flops=2 * rows * feats * cols, bytes_accessed=2 * (rows * cols + feats * cols + rows * feats))
    if take is None:
        kernel = functools.partial(grad_in_kernel, n=len(flat), parts=parts)
        out = pl.BlockSpec((rows, tile), lambda i: (0, i))
        return call(kernel, (feats // tile,), specs, out, jax.ShapeDtypeStruct((rows, feats), BF16), **cost)(*flat, weight)
    n_out = take.shape[1]
    kernel = functools.partial(grad_in_sorted_kernel, n=len(flat), parts=parts, n_out=n_out, half=half)
    outs = [pl.BlockSpec((half, tile), lambda i, *_: (0, i))] * n_out
    shapes = [jax.ShapeDtypeStruct((half, feats), BF16)] * n_out
    return call(kernel, (feats // tile,), specs, outs, shapes, scalars=(me, take), **cost)(
        me, jnp.asarray(take.reshape(-1), jnp.int32), *flat, weight
    )


def assemble(dst, refs):
    at = 0
    for r in refs:
        dst[at : at + r.shape[0], :] = r[...]
        at += r.shape[0]


def pass_kernel(_, __, *refs, n, n_grads, last, n_old, rows):
    attn, grads, rest = refs[:n], refs[n : n + n_grads], refs[n + n_grads :]
    if last:
        acc_ref, w_ref = rest[:2]
        new_w, new_m, attn_s, grad_s = rest[2 + n_old :]
    else:
        m_ref, out, attn_s, grad_s = rest

    @pl.when(pl.program_id(0) == 0)
    def _():
        assemble(attn_s, attn)

    assemble(grad_s, grads)
    for c in range(0, attn_s.shape[1], rows):
        here = slice(c, c + rows)
        add = lax.dot_general(attn_s[:, here], grad_s[...], TN, preferred_element_type=F32)
        if last:
            mom = acc_ref[here].astype(F32) + add
            new_w[here] = (w_ref[here].astype(F32) - 0.25 * mom).astype(BF16)
            new_m[here] = mom.astype(BF16)
        else:
            out[here] = (0.9 * m_ref[here].astype(F32) + add).astype(out.dtype)


def token_pass(me, order, attn_all, pieces, wides, first_col=0, n_cols=None, old=(), out_dtype=None, tile=512):
    last = len(wides) == 2
    n = len(pieces)
    half = pieces[0][0].shape[0]
    feats, cols = wides[0].shape
    n_cols = n_cols or cols
    tile = fit(n_cols, tile)
    base = first_col // tile
    specs = [pl.BlockSpec((half, feats), lambda j, me, o, i=i: (o[me[0] * n + i], 0)) for i in range(n)]
    specs += [pl.BlockSpec((half, tile), lambda j, *_, c=(first_col - at) // tile: (0, j + c)) for _, at in pieces]
    wide = pl.BlockSpec((feats, tile), lambda j, *_: (0, j + base))
    specs += [wide] * len(wides) + [pl.BlockSpec(memory_space=pl.ANY)] * len(old)
    shape = jax.ShapeDtypeStruct((feats, cols), BF16 if last else out_dtype)
    return call(
        functools.partial(pass_kernel, n=n, n_grads=n, last=last, n_old=len(old), rows=fit(feats, 512)),
        (n_cols // tile,),
        specs,
        [wide, wide] if last else wide,
        [shape, shape] if last else shape,
        scalars=(me, order),
        scratch=[pltpu.VMEM((n * half, feats), BF16), pltpu.VMEM((n * half, tile), BF16)],
        aliases={2 + 2 * n + 2 + i: i for i in range(len(old))},
        flops=2 * n * half * feats * n_cols,
        bytes_accessed=8 * feats * n_cols,
    )(me, jnp.asarray(order.reshape(-1), jnp.int32), *([attn_all] * n), *[x for x, _ in pieces], *wides, *old)


def pair_sum_kernel(_, __, *refs, n):
    ins, outs = refs[: 2 * n], refs[2 * n :]
    for s in range(n):
        outs[s][...] = (ins[2 * s][...].astype(F32) + ins[2 * s + 1][...].astype(F32)).astype(BF16)


def pair_sum(me, which, mine, other, half, tile=512):
    n, width = which.shape[1], mine.shape[1]
    tile = fit(width, tile)
    picked = [pl.BlockSpec((half, tile), lambda i, me, w, s=s: (w[me[0] * n + s], i)) for s in range(n) for _ in range(2)]
    return call(
        functools.partial(pair_sum_kernel, n=n),
        (width // tile,),
        picked,
        [pl.BlockSpec((half, tile), lambda i, *_: (0, i))] * n,
        [jax.ShapeDtypeStruct((half, width), BF16)] * n,
        scalars=(me, which),
        vmem=SUM_VMEM,
        bytes_accessed=6 * n * half * width,
    )(me, jnp.asarray(which.reshape(-1), jnp.int32), *([mine, other] * n))


def place_kernel(me, _, valid, __, *refs, spans, total_slots):
    out, i = refs[-1], pl.program_id(0)
    flag = valid[me[0] * total_slots + i]
    at = 0
    for counts, n_picked in spans:
        picked = refs[at : at + n_picked]
        at += n_picked
        for slot, n_received in counts:
            mine = [*picked, *refs[at : at + n_received]]
            at += n_received

            @pl.when((flag == 1) & (i == slot))
            def _():
                total = mine[0][...].astype(F32)
                for r in mine[1:]:
                    total = total + r[...].astype(F32)
                out[...] = total.astype(BF16)

    if len(refs) > at + 1:

        @pl.when(flag == 2)
        def _():
            out[...] = refs[at][...]


def place(me, groups, out, shape, half):
    which = np.concatenate([g[0][0] for g in groups], axis=1)
    valid = np.concatenate([g[0][1] for g in groups], axis=1)
    where = np.concatenate([g[0][2] for g in groups], axis=1)
    n = which.shape[1]
    for d in range(len(valid)):
        real = np.flatnonzero(valid[d])
        if len(real) == 0:
            valid[d], where[d] = 2, 0
            continue
        for s in range(n):
            before = real[real <= s]
            near = before[-1] if len(before) else real[0]
            where[d, s] = where[d, near]
    width = shape[1]
    specs, args, spans, first = [], [], [], 0
    for tables, picked, received in groups:
        slots = tables[0].shape[1]
        at = lambda i, f=first, s=slots: jnp.clip(i, f, f + s - 1)
        specs += [pl.BlockSpec((half, width), lambda i, me, w, v, p, at=at: (w[me[0] * n + at(i)], 0)) for _ in picked]
        args += picked
        for r in received:
            specs += [pl.BlockSpec((half, width), lambda i, *_: (0, 0)) for _ in r]
            args += r
        spans.append(([(first + s, len(r)) for s, r in enumerate(received)], len(picked)))
        first += slots
    spec = pl.BlockSpec((half, width), lambda i, me, w, v, p: (p[me[0] * n + i], 0))
    aliases = {}
    kernel = functools.partial(place_kernel, spans=spans, total_slots=n)
    if out is not None:
        keep = (valid == 2).any()
        specs.append(spec if keep else pl.BlockSpec(memory_space=pl.ANY))
        args.append(out)
        aliases = {4 + len(args) - 1: 0}
        if not keep:
            inner = kernel
            kernel = lambda *refs: inner(*refs[:-2], refs[-1])
    return call(
        kernel,
        (n,),
        specs,
        spec,
        jax.ShapeDtypeStruct(shape, BF16),
        scalars=(me, which, valid, where),
        aliases=aliases,
        bytes_accessed=8 * n * half * width,
    )(me, *[jnp.asarray(t.reshape(-1), jnp.int32) for t in (which, valid, where)], *args)


def body(n_row, n_col, attn, grad_out, weight, momentum):
    ring = np.array(snake(n_row))
    pos = np.argsort(ring)
    right = [(int(ring[i]), int(ring[(i + 1) % n_row])) for i in range(n_row)]
    left = [(b, a) for a, b in right]
    block, cols = grad_out.shape
    half = block // 2
    per_owner = n_row // n_col
    n_y = n_col // 2
    devices = [(r, c) for r in range(n_row) for c in range(n_col)]
    me = (lax.axis_index("row") * n_col + lax.axis_index("col")).astype(jnp.int32).reshape(1)
    out_shape = (per_owner * block, weight.shape[0])

    arrives = np.zeros((n_row, n_row, 2), np.int32)
    for r in range(n_row):
        for k in range(n_row):
            arrives[r, k, 0] = 2 * ring[(pos[r] - k) % n_row]
            arrives[r, k, 1] = 2 * ring[(pos[r] + k) % n_row] + 1

    held = np.zeros((n_row * n_col, 2 * n_row), np.int32)
    for d, (r, c) in enumerate(devices):
        near = [(c + s) % n_col for s in range(0, n_col, 2)]
        for at, owner in enumerate(near + [o ^ 1 for o in near]):
            held[d, owner * 2 * per_owner : (owner + 1) * 2 * per_owner] = np.arange(2 * per_owner) + at * 2 * per_owner

    def order_of(steps):
        return np.stack([held[d, arrives[r, np.array(steps)].reshape(-1)] for d, (r, _) in enumerate(devices)])

    def tables_of(steps):
        halves = arrives[:, np.array(steps), :].reshape(n_row, -1)
        owner = halves // (2 * per_owner)
        slots = max(int(np.sum(owner[r] == c)) for r, c in devices)
        which, valid, where = (np.zeros((n_row * n_col, slots), np.int32) for _ in range(3))
        for d, (r, c) in enumerate(devices):
            own = np.flatnonzero(owner[r] == c)
            spots = list(halves[r, own] % (2 * per_owner))
            spots += [s for s in range(2 * per_owner) if s not in spots]
            which[d, : len(own)] = own
            valid[d, : len(own)] = 1
            where[d] = spots[:slots]
        return which, valid, where

    def route(valid, shift, slot):
        to = [(r, (c + shift) % n_col) for r, c in devices]
        return [(d, r * n_col + c) for d, (r, c) in enumerate(to) if valid[r * n_col + c, slot]]

    cores = [(c, c ^ 1) for c in range(n_col)]

    def send(arrays, valid, shift):
        return [lax.ppermute(x, ("row", "col"), route(valid, shift, s)) for s, x in enumerate(arrays)]

    def shifted(table, shift):
        return np.stack([table[r * n_col + (c + shift) % n_col] for r, c in devices])

    def reduce_in_pairs(steps, part, wait=0, hold=0, late=0):
        tables = tables_of(steps)
        for _ in range(wait):
            yield ()
        other = lax.ppermute(part, "col", cores)
        shifts = range(2, n_col, 2)
        sums = [pair_sum(me, shifted(tables[0], s), part, other, half) for s in shifts]
        other, sums = yield other, sums
        for _ in range(hold):
            yield ()
        received = [send(sums[i], tables[1], s) for i, s in enumerate(shifts)]
        for _ in range(late):
            yield ()
        received = yield received
        done.append((tables, [part, other], [list(r) for r in zip(*received)]))

    def reduce_direct(step, parts):
        tables = tables_of([step])
        received = yield [send([parts[s]], tables[1], s)[0] for s in range(1, n_col)]
        done.append((tables, [], [[parts[0], *received]]))

    def sorted_part(step):
        which = tables_of([step])[0]
        take = np.concatenate([shifted(which, s) for s in range(n_col)], axis=1)
        return grad_in_part(pieces_of([step]), weight, take, me)

    arrived = {0: (grad_out[:half], grad_out[half:])}
    pieces_of = lambda steps: [(x,) for k in steps for x in arrived[k]]
    whole_pieces = lambda steps: [(x, 0) for k in steps for x in arrived[k]]

    top = n_row - 1
    mid = n_row // 2
    early = list(range(0, mid - 1))
    late = list(range(mid - 1, n_row))
    at_work = {
        1: ([0], 0, 0, 0),
        2: ([1], 2, 0, 0),
        mid - 1: (list(range(2, mid - 1)), 1, 0, 0),
        mid + 1: ([mid - 1, mid], 0, 0, 0),
        top - 1: (list(range(mid + 1, top - 1)), 0, 0, 0),
        top: ([top - 1], 0, 0, 0),
    }
    done, moving = [], []
    acc = grad_in = None

    def turn(on_link, work):
        nonlocal moving
        on_link, work, flights = tie(on_link, work, [f for _, f in moving])
        moving = [[g, f] for (g, _), f in zip(moving, flights)]
        return on_link, work

    def advance():
        nonlocal moving
        still = []
        for g, f in moving:
            try:
                still.append([g, g.send(f)])
            except StopIteration:
                pass
        moving = still

    def begin(g):
        moving.append([g, next(g)])

    for k in range(1, n_row):
        a, b = arrived[k - 1]
        nxt = (lax.ppermute(a, "row", right), lax.ppermute(b, "row", left))
        work = ()
        if k in at_work:
            work = grad_in_part(pieces_of(at_work[k][0]), weight)
        elif k == mid:
            work = token_pass(me, order_of(early), attn_all, whole_pieces(early), (momentum,), out_dtype=BF16)
        extra = ()
        if k == 1:
            far = [lax.ppermute(attn, "col", [(c, (c - s) % n_col) for c in range(n_col)]) for s in range(2, n_col, 2)]
            extra = lax.ppermute(attn, "col", cores)
        elif k == 2:
            extra = far
        elif k == 3:
            extra = jnp.concatenate([attn, *far, beside, *[lax.ppermute(x, "col", cores) for x in far]])
        elif k == top and done:
            extra = place(me, done, None, out_shape, half)
            done.clear()
        arrived[k], (work, extra) = turn(nxt, (work, extra))
        if k == 1:
            beside = extra
        elif k == 2:
            far = extra
        elif k == 3:
            attn_all = extra
        elif k == top and not isinstance(extra, tuple):
            grad_in = extra
        advance()
        if k in at_work:
            begin(reduce_in_pairs(at_work[k][0], work, *at_work[k][1:]))
        elif k == mid:
            acc = work
    parts = sorted_part(top)
    sums = [f for g, f in moving if len(f) == 2 and not isinstance(f, list)]
    parts, acc, sums = tie(parts, acc, sums)
    sums = iter(sums)
    moving = [[g, next(sums) if len(f) == 2 and not isinstance(f, list) else f] for g, f in moving]
    still = []
    for g, f in moving:
        still.append([g, g.send(f)] if not isinstance(f, list) else [g, f])
    moving = still
    begin(reduce_direct(top, parts))
    new_w, new_m = token_pass(me, order_of(late), attn_all, whole_pieces(late), (acc, weight))
    _, (new_w, new_m) = turn((), (new_w, new_m))
    while moving:
        advance()
    grad_in = place(me, done, grad_in, out_shape, half)
    return grad_in, new_w, new_m


def solution(mesh):
    n_row, n_col = mesh.shape["row"], mesh.shape["col"]
    spec, act = P("row", "col"), P("col", "row")

    def shards(attn, grad_out, weight, momentum):
        return body(n_row, n_col, attn, grad_out, weight, momentum)

    return jax.shard_map(shards, mesh=mesh, in_specs=(act, spec, spec, spec), out_specs=(act, spec, spec), check_vma=False)
```

```python
import functools

import jax
import jax.numpy as jnp
import numpy as np
from jax import lax
from jax.experimental import pallas as pl
from jax.experimental.pallas import tpu as pltpu
from jax.sharding import PartitionSpec as P

BF16 = jnp.bfloat16
F32 = jnp.float32
NT = (((1,), (1,)), ((), ()))
TN = (((0,), (0,)), ((), ()))
VMEM_BYTES = 60 << 20
GRAD_IN_VMEM, SUM_VMEM = 50 << 20, 24 << 20


def snake(n):
    return list(range(0, n, 2)) + list(range(n - 1 - (n % 2), 0, -2))


def tie(*xs):
    return lax.optimization_barrier(xs)


def fit(size, want):
    while size % want:
        want //= 2
    return want


def call(kernel, grid, in_specs, out_specs, out_shape, scalars=(), scratch=(), aliases=None, flops=0, bytes_accessed=0, vmem=VMEM_BYTES):
    return pl.pallas_call(
        kernel,
        grid_spec=pltpu.PrefetchScalarGridSpec(
            num_scalar_prefetch=len(scalars), grid=grid, in_specs=in_specs, out_specs=out_specs, scratch_shapes=scratch
        ),
        out_shape=out_shape,
        input_output_aliases=aliases or {},
        compiler_params=pltpu.CompilerParams(vmem_limit_bytes=vmem),
        cost_estimate=pl.CostEstimate(flops=flops, bytes_accessed=bytes_accessed, transcendentals=0),
    )


def tokens_of(refs, parts):
    halves = [refs[i : i + parts] for i in range(0, len(refs), parts)]
    rows = [h[0][...] if parts == 1 else jnp.concatenate([r[...] for r in h], axis=1) for h in halves]
    return jnp.concatenate(rows)


def grad_in_kernel(*refs, n, parts):
    total = lax.dot_general(tokens_of(refs[:n], parts), refs[n][...], NT, preferred_element_type=F32)
    refs[-1][...] = total.astype(BF16)


def grad_in_sorted_kernel(me, take, *refs, n, parts, n_out, half):
    total = lax.dot_general(tokens_of(refs[:n], parts), refs[n][...], NT, preferred_element_type=F32).astype(BF16)
    for s in range(n_out):
        upper = take[me[0] * n_out + s] > 0
        refs[n + 1 + s][...] = jnp.where(upper, total[half:], total[:half])


def grad_in_part(pieces, weight, take=None, me=None, tile=512):
    parts, half = len(pieces[0]), pieces[0][0].shape[0]
    feats, cols = weight.shape
    rows = half * len(pieces)
    tile = fit(feats, tile if rows > 2 * half else 2 * tile)
    flat = [x for p in pieces for x in p]
    specs = [pl.BlockSpec(x.shape, lambda i, *_: (0, 0)) for x in flat]
    specs.append(pl.BlockSpec((tile, cols), lambda i, *_: (i, 0)))
    cost = dict(vmem=GRAD_IN_VMEM, flops=2 * rows * feats * cols, bytes_accessed=2 * (rows * cols + feats * cols + rows * feats))
    if take is None:
        kernel = functools.partial(grad_in_kernel, n=len(flat), parts=parts)
        out = pl.BlockSpec((rows, tile), lambda i: (0, i))
        return call(kernel, (feats // tile,), specs, out, jax.ShapeDtypeStruct((rows, feats), BF16), **cost)(*flat, weight)
    n_out = take.shape[1]
    kernel = functools.partial(grad_in_sorted_kernel, n=len(flat), parts=parts, n_out=n_out, half=half)
    outs = [pl.BlockSpec((half, tile), lambda i, *_: (0, i))] * n_out
    shapes = [jax.ShapeDtypeStruct((half, feats), BF16)] * n_out
    return call(kernel, (feats // tile,), specs, outs, shapes, scalars=(me, take), **cost)(
        me, jnp.asarray(take.reshape(-1), jnp.int32), *flat, weight
    )


def assemble(dst, refs):
    at = 0
    for r in refs:
        dst[at : at + r.shape[0], :] = r[...]
        at += r.shape[0]


def pass_kernel(_, __, *refs, n, n_grads, last, n_old, rows):
    attn, grads, rest = refs[:n], refs[n : n + n_grads], refs[n + n_grads :]
    if last:
        acc_ref, w_ref = rest[:2]
        new_w, new_m, attn_s, grad_s = rest[2 + n_old :]
    else:
        m_ref, out, attn_s, grad_s = rest

    @pl.when(pl.program_id(0) == 0)
    def _():
        assemble(attn_s, attn)

    assemble(grad_s, grads)
    for c in range(0, attn_s.shape[1], rows):
        here = slice(c, c + rows)
        add = lax.dot_general(attn_s[:, here], grad_s[...], TN, preferred_element_type=F32)
        if last:
            mom = acc_ref[here].astype(F32) + add
            new_w[here] = (w_ref[here].astype(F32) - 0.25 * mom).astype(BF16)
            new_m[here] = mom.astype(BF16)
        else:
            out[here] = (0.9 * m_ref[here].astype(F32) + add).astype(out.dtype)


def token_pass(me, order, attn_all, pieces, wides, first_col=0, n_cols=None, old=(), out_dtype=None, tile=512):
    last = len(wides) == 2
    n = len(pieces)
    half = pieces[0][0].shape[0]
    feats, cols = wides[0].shape
    n_cols = n_cols or cols
    tile = fit(n_cols, tile)
    base = first_col // tile
    specs = [pl.BlockSpec((half, feats), lambda j, me, o, i=i: (o[me[0] * n + i], 0)) for i in range(n)]
    specs += [pl.BlockSpec((half, tile), lambda j, *_, c=(first_col - at) // tile: (0, j + c)) for _, at in pieces]
    wide = pl.BlockSpec((feats, tile), lambda j, *_: (0, j + base))
    specs += [wide] * len(wides) + [pl.BlockSpec(memory_space=pl.ANY)] * len(old)
    shape = jax.ShapeDtypeStruct((feats, cols), BF16 if last else out_dtype)
    return call(
        functools.partial(pass_kernel, n=n, n_grads=n, last=last, n_old=len(old), rows=fit(feats, 512)),
        (n_cols // tile,),
        specs,
        [wide, wide] if last else wide,
        [shape, shape] if last else shape,
        scalars=(me, order),
        scratch=[pltpu.VMEM((n * half, feats), BF16), pltpu.VMEM((n * half, tile), BF16)],
        aliases={2 + 2 * n + 2 + i: i for i in range(len(old))},
        flops=2 * n * half * feats * n_cols,
        bytes_accessed=8 * feats * n_cols,
    )(me, jnp.asarray(order.reshape(-1), jnp.int32), *([attn_all] * n), *[x for x, _ in pieces], *wides, *old)


def pair_sum_kernel(_, __, *refs, n):
    ins, outs = refs[: 2 * n], refs[2 * n :]
    for s in range(n):
        outs[s][...] = (ins[2 * s][...].astype(F32) + ins[2 * s + 1][...].astype(F32)).astype(BF16)


def pair_sum(me, which, mine, other, half, tile=512):
    n, width = which.shape[1], mine.shape[1]
    tile = fit(width, tile)
    picked = [pl.BlockSpec((half, tile), lambda i, me, w, s=s: (w[me[0] * n + s], i)) for s in range(n) for _ in range(2)]
    return call(
        functools.partial(pair_sum_kernel, n=n),
        (width // tile,),
        picked,
        [pl.BlockSpec((half, tile), lambda i, *_: (0, i))] * n,
        [jax.ShapeDtypeStruct((half, width), BF16)] * n,
        scalars=(me, which),
        vmem=SUM_VMEM,
        bytes_accessed=6 * n * half * width,
    )(me, jnp.asarray(which.reshape(-1), jnp.int32), *([mine, other] * n))


def place_kernel(me, _, valid, __, *refs, spans, total_slots):
    out, i = refs[-1], pl.program_id(0)
    flag = valid[me[0] * total_slots + i]
    at = 0
    for counts, n_picked in spans:
        picked = refs[at : at + n_picked]
        at += n_picked
        for slot, n_received in counts:
            mine = [*picked, *refs[at : at + n_received]]
            at += n_received

            @pl.when((flag == 1) & (i == slot))
            def _():
                total = mine[0][...].astype(F32)
                for r in mine[1:]:
                    total = total + r[...].astype(F32)
                out[...] = total.astype(BF16)

    if len(refs) > at + 1:

        @pl.when(flag == 2)
        def _():
            out[...] = refs[at][...]


def place(me, groups, out, shape, half):
    which = np.concatenate([g[0][0] for g in groups], axis=1)
    valid = np.concatenate([g[0][1] for g in groups], axis=1)
    where = np.concatenate([g[0][2] for g in groups], axis=1)
    n = which.shape[1]
    for d in range(len(valid)):
        real = np.flatnonzero(valid[d])
        if len(real) == 0:
            valid[d], where[d] = 2, 0
            continue
        for s in range(n):
            before = real[real <= s]
            near = before[-1] if len(before) else real[0]
            where[d, s] = where[d, near]
    width = shape[1]
    specs, args, spans, first = [], [], [], 0
    for tables, picked, received in groups:
        slots = tables[0].shape[1]
        at = lambda i, f=first, s=slots: jnp.clip(i, f, f + s - 1)
        specs += [pl.BlockSpec((half, width), lambda i, me, w, v, p, at=at: (w[me[0] * n + at(i)], 0)) for _ in picked]
        args += picked
        for r in received:
            specs += [pl.BlockSpec((half, width), lambda i, *_: (0, 0)) for _ in r]
            args += r
        spans.append(([(first + s, len(r)) for s, r in enumerate(received)], len(picked)))
        first += slots
    spec = pl.BlockSpec((half, width), lambda i, me, w, v, p: (p[me[0] * n + i], 0))
    aliases = {}
    kernel = functools.partial(place_kernel, spans=spans, total_slots=n)
    if out is not None:
        keep = (valid == 2).any()
        specs.append(spec if keep else pl.BlockSpec(memory_space=pl.ANY))
        args.append(out)
        aliases = {4 + len(args) - 1: 0}
        if not keep:
            inner = kernel
            kernel = lambda *refs: inner(*refs[:-2], refs[-1])
    return call(
        kernel,
        (n,),
        specs,
        spec,
        jax.ShapeDtypeStruct(shape, BF16),
        scalars=(me, which, valid, where),
        aliases=aliases,
        bytes_accessed=8 * n * half * width,
    )(me, *[jnp.asarray(t.reshape(-1), jnp.int32) for t in (which, valid, where)], *args)


def body(n_row, n_col, attn, grad_out, weight, momentum):
    ring = np.array(snake(n_row))
    pos = np.argsort(ring)
    right = [(int(ring[i]), int(ring[(i + 1) % n_row])) for i in range(n_row)]
    left = [(b, a) for a, b in right]
    block, cols = grad_out.shape
    half = block // 2
    per_owner = n_row // n_col
    n_y = n_col // 2
    devices = [(r, c) for r in range(n_row) for c in range(n_col)]
    me = (lax.axis_index("row") * n_col + lax.axis_index("col")).astype(jnp.int32).reshape(1)
    out_shape = (per_owner * block, weight.shape[0])

    arrives = np.zeros((n_row, n_row, 2), np.int32)
    for r in range(n_row):
        for k in range(n_row):
            arrives[r, k, 0] = 2 * ring[(pos[r] - k) % n_row]
            arrives[r, k, 1] = 2 * ring[(pos[r] + k) % n_row] + 1

    held = np.zeros((n_row * n_col, 2 * n_row), np.int32)
    for d, (r, c) in enumerate(devices):
        near = [(c + s) % n_col for s in range(0, n_col, 2)]
        for at, owner in enumerate(near + [o ^ 1 for o in near]):
            held[d, owner * 2 * per_owner : (owner + 1) * 2 * per_owner] = np.arange(2 * per_owner) + at * 2 * per_owner

    def order_of(steps):
        return np.stack([held[d, arrives[r, np.array(steps)].reshape(-1)] for d, (r, _) in enumerate(devices)])

    def tables_of(steps):
        halves = arrives[:, np.array(steps), :].reshape(n_row, -1)
        owner = halves // (2 * per_owner)
        slots = max(int(np.sum(owner[r] == c)) for r, c in devices)
        which, valid, where = (np.zeros((n_row * n_col, slots), np.int32) for _ in range(3))
        for d, (r, c) in enumerate(devices):
            own = np.flatnonzero(owner[r] == c)
            spots = list(halves[r, own] % (2 * per_owner))
            spots += [s for s in range(2 * per_owner) if s not in spots]
            which[d, : len(own)] = own
            valid[d, : len(own)] = 1
            where[d] = spots[:slots]
        return which, valid, where

    def route(valid, shift, slot):
        to = [(r, (c + shift) % n_col) for r, c in devices]
        return [(d, r * n_col + c) for d, (r, c) in enumerate(to) if valid[r * n_col + c, slot]]

    cores = [(c, c ^ 1) for c in range(n_col)]

    def send(arrays, valid, shift):
        return [lax.ppermute(x, ("row", "col"), route(valid, shift, s)) for s, x in enumerate(arrays)]

    def shifted(table, shift):
        return np.stack([table[r * n_col + (c + shift) % n_col] for r, c in devices])

    def reduce_in_pairs(steps, part, wait=0, hold=0, late=0):
        tables = tables_of(steps)
        for _ in range(wait):
            yield ()
        other = lax.ppermute(part, "col", cores)
        shifts = range(2, n_col, 2)
        sums = [pair_sum(me, shifted(tables[0], s), part, other, half) for s in shifts]
        other, sums = yield other, sums
        for _ in range(hold):
            yield ()
        received = [send(sums[i], tables[1], s) for i, s in enumerate(shifts)]
        for _ in range(late):
            yield ()
        received = yield received
        done.append((tables, [part, other], [list(r) for r in zip(*received)]))

    def reduce_direct(step, parts):
        tables = tables_of([step])
        received = yield [send([parts[s]], tables[1], s)[0] for s in range(1, n_col)]
        done.append((tables, [], [[parts[0], *received]]))

    def sorted_part(step):
        which = tables_of([step])[0]
        take = np.concatenate([shifted(which, s) for s in range(n_col)], axis=1)
        return grad_in_part(pieces_of([step]), weight, take, me)

    arrived = {0: (grad_out[:half], grad_out[half:])}
    pieces_of = lambda steps: [(x,) for k in steps for x in arrived[k]]
    whole_pieces = lambda steps: [(x, 0) for k in steps for x in arrived[k]]

    top = n_row - 1
    mid = n_row // 2
    early = list(range(0, mid - 1))
    late = list(range(mid - 1, n_row))
    at_work = {
        1: ([0], 0, 2, 0),
        2: ([1], 2, 0, 0),
        mid - 1: (list(range(2, mid - 1)), 1, 0, 0),
        mid + 1: ([mid - 1, mid], 0, 0, 0),
        top - 1: (list(range(mid + 1, top - 1)), 0, 0, 0),
        top: ([top - 1], 0, 0, 0),
    }
    done, moving = [], []
    acc = grad_in = None

    def turn(on_link, work):
        nonlocal moving
        on_link, work, flights = tie(on_link, work, [f for _, f in moving])
        moving = [[g, f] for (g, _), f in zip(moving, flights)]
        return on_link, work

    def advance():
        nonlocal moving
        still = []
        for g, f in moving:
            try:
                still.append([g, g.send(f)])
            except StopIteration:
                pass
        moving = still

    def begin(g):
        moving.append([g, next(g)])

    for k in range(1, n_row):
        a, b = arrived[k - 1]
        nxt = (lax.ppermute(a, "row", right), lax.ppermute(b, "row", left))
        work = ()
        if k in at_work:
            work = grad_in_part(pieces_of(at_work[k][0]), weight)
        elif k == mid:
            work = token_pass(me, order_of(early), attn_all, whole_pieces(early), (momentum,), out_dtype=BF16, tile=1024)
        extra = ()
        if k == 1:
            far = [lax.ppermute(attn, "col", [(c, (c - s) % n_col) for c in range(n_col)]) for s in range(2, n_col, 2)]
            extra = lax.ppermute(attn, "col", cores)
        elif k == 2:
            extra = far
        elif k == 3:
            extra = jnp.concatenate([attn, *far, beside, *[lax.ppermute(x, "col", cores) for x in far]])
        elif k == top and done:
            extra = place(me, done, None, out_shape, half)
            done.clear()
        arrived[k], (work, extra) = turn(nxt, (work, extra))
        if k == 1:
            beside = extra
        elif k == 2:
            far = extra
        elif k == 3:
            attn_all = extra
        elif k == top and not isinstance(extra, tuple):
            grad_in = extra
        advance()
        if k in at_work:
            begin(reduce_in_pairs(at_work[k][0], work, *at_work[k][1:]))
        elif k == mid:
            acc = work
    parts = sorted_part(top)
    sums = [f for g, f in moving if len(f) == 2 and not isinstance(f, list)]
    parts, acc, sums = tie(parts, acc, sums)
    sums = iter(sums)
    moving = [[g, next(sums) if len(f) == 2 and not isinstance(f, list) else f] for g, f in moving]
    still = []
    for g, f in moving:
        still.append([g, g.send(f)] if not isinstance(f, list) else [g, f])
    moving = still
    begin(reduce_direct(top, parts))
    new_w, new_m = token_pass(me, order_of(late), attn_all, whole_pieces(late), (acc, weight))
    _, (new_w, new_m) = turn((), (new_w, new_m))
    while moving:
        advance()
    grad_in = place(me, done, grad_in, out_shape, half)
    return grad_in, new_w, new_m


def solution(mesh):
    n_row, n_col = mesh.shape["row"], mesh.shape["col"]
    spec, act = P("row", "col"), P("col", "row")

    def shards(attn, grad_out, weight, momentum):
        return body(n_row, n_col, attn, grad_out, weight, momentum)

    return jax.shard_map(shards, mesh=mesh, in_specs=(act, spec, spec, spec), out_specs=(act, spec, spec), check_vma=False)
```

```python
import functools

import jax
import jax.numpy as jnp
import numpy as np
from jax import lax
from jax.experimental import pallas as pl
from jax.experimental.pallas import tpu as pltpu
from jax.sharding import PartitionSpec as P

BF16 = jnp.bfloat16
F32 = jnp.float32
NT = (((1,), (1,)), ((), ()))
TN = (((0,), (0,)), ((), ()))
VMEM_BYTES = 60 << 20
GRAD_IN_VMEM, SUM_VMEM, LAST_VMEM = 50 << 20, 24 << 20, 46 << 20


def snake(n):
    return list(range(0, n, 2)) + list(range(n - 1 - (n % 2), 0, -2))


def tie(*xs):
    return lax.optimization_barrier(xs)


def fit(size, want):
    while size % want:
        want //= 2
    return want


def call(kernel, grid, in_specs, out_specs, out_shape, scalars=(), scratch=(), aliases=None, flops=0, bytes_accessed=0, vmem=VMEM_BYTES):
    return pl.pallas_call(
        kernel,
        grid_spec=pltpu.PrefetchScalarGridSpec(
            num_scalar_prefetch=len(scalars), grid=grid, in_specs=in_specs, out_specs=out_specs, scratch_shapes=scratch
        ),
        out_shape=out_shape,
        input_output_aliases=aliases or {},
        compiler_params=pltpu.CompilerParams(vmem_limit_bytes=vmem),
        cost_estimate=pl.CostEstimate(flops=flops, bytes_accessed=bytes_accessed, transcendentals=0),
    )


def tokens_of(refs, parts):
    halves = [refs[i : i + parts] for i in range(0, len(refs), parts)]
    rows = [h[0][...] if parts == 1 else jnp.concatenate([r[...] for r in h], axis=1) for h in halves]
    return jnp.concatenate(rows)


def grad_in_kernel(*refs, n, parts):
    total = lax.dot_general(tokens_of(refs[:n], parts), refs[n][...], NT, preferred_element_type=F32)
    refs[-1][...] = total.astype(BF16)


def grad_in_sorted_kernel(me, take, *refs, n, parts, n_out, half):
    total = lax.dot_general(tokens_of(refs[:n], parts), refs[n][...], NT, preferred_element_type=F32).astype(BF16)
    for s in range(n_out):
        upper = take[me[0] * n_out + s] > 0
        refs[n + 1 + s][...] = jnp.where(upper, total[half:], total[:half])


def grad_in_part(pieces, weight, take=None, me=None, tile=512):
    parts, half = len(pieces[0]), pieces[0][0].shape[0]
    feats, cols = weight.shape
    rows = half * len(pieces)
    tile = fit(feats, tile if rows > 2 * half else 2 * tile)
    flat = [x for p in pieces for x in p]
    specs = [pl.BlockSpec(x.shape, lambda i, *_: (0, 0)) for x in flat]
    specs.append(pl.BlockSpec((tile, cols), lambda i, *_: (i, 0)))
    cost = dict(vmem=GRAD_IN_VMEM, flops=2 * rows * feats * cols, bytes_accessed=2 * (rows * cols + feats * cols + rows * feats))
    if take is None:
        kernel = functools.partial(grad_in_kernel, n=len(flat), parts=parts)
        out = pl.BlockSpec((rows, tile), lambda i: (0, i))
        return call(kernel, (feats // tile,), specs, out, jax.ShapeDtypeStruct((rows, feats), BF16), **cost)(*flat, weight)
    n_out = take.shape[1]
    kernel = functools.partial(grad_in_sorted_kernel, n=len(flat), parts=parts, n_out=n_out, half=half)
    outs = [pl.BlockSpec((half, tile), lambda i, *_: (0, i))] * n_out
    shapes = [jax.ShapeDtypeStruct((half, feats), BF16)] * n_out
    return call(kernel, (feats // tile,), specs, outs, shapes, scalars=(me, take), **cost)(
        me, jnp.asarray(take.reshape(-1), jnp.int32), *flat, weight
    )


def assemble(dst, refs):
    at = 0
    for r in refs:
        dst[at : at + r.shape[0], :] = r[...]
        at += r.shape[0]


def pass_kernel(_, __, *refs, n, n_grads, last, n_old, rows):
    attn, grads, rest = refs[:n], refs[n : n + n_grads], refs[n + n_grads :]
    if last:
        acc_ref, w_ref = rest[:2]
        new_w, new_m, attn_s, grad_s = rest[2 + n_old :]
    else:
        m_ref, out, attn_s, grad_s = rest

    @pl.when(pl.program_id(0) == 0)
    def _():
        assemble(attn_s, attn)

    assemble(grad_s, grads)
    for c in range(0, attn_s.shape[1], rows):
        here = slice(c, c + rows)
        add = lax.dot_general(attn_s[:, here], grad_s[...], TN, preferred_element_type=F32)
        if last:
            mom = acc_ref[here].astype(F32) + add
            new_w[here] = (w_ref[here].astype(F32) - 0.25 * mom).astype(BF16)
            new_m[here] = mom.astype(BF16)
        else:
            out[here] = (0.9 * m_ref[here].astype(F32) + add).astype(out.dtype)


def token_pass(me, order, attn_all, pieces, wides, first_col=0, n_cols=None, old=(), out_dtype=None, tile=512):
    last = len(wides) == 2
    n = len(pieces)
    half = pieces[0][0].shape[0]
    feats, cols = wides[0].shape
    n_cols = n_cols or cols
    tile = fit(n_cols, tile)
    base = first_col // tile
    specs = [pl.BlockSpec((half, feats), lambda j, me, o, i=i: (o[me[0] * n + i], 0)) for i in range(n)]
    specs += [pl.BlockSpec((half, tile), lambda j, *_, c=(first_col - at) // tile: (0, j + c)) for _, at in pieces]
    wide = pl.BlockSpec((feats, tile), lambda j, *_: (0, j + base))
    specs += [wide] * len(wides) + [pl.BlockSpec(memory_space=pl.ANY)] * len(old)
    shape = jax.ShapeDtypeStruct((feats, cols), BF16 if last else out_dtype)
    return call(
        functools.partial(pass_kernel, n=n, n_grads=n, last=last, n_old=len(old), rows=fit(feats, 512)),
        (n_cols // tile,),
        specs,
        [wide, wide] if last else wide,
        [shape, shape] if last else shape,
        scalars=(me, order),
        scratch=[pltpu.VMEM((n * half, feats), BF16), pltpu.VMEM((n * half, tile), BF16)],
        aliases={2 + 2 * n + 2 + i: i for i in range(len(old))},
        vmem=LAST_VMEM if last else VMEM_BYTES,
        flops=2 * n * half * feats * n_cols,
        bytes_accessed=8 * feats * n_cols,
    )(me, jnp.asarray(order.reshape(-1), jnp.int32), *([attn_all] * n), *[x for x, _ in pieces], *wides, *old)


def pair_sum_kernel(_, __, *refs, n):
    ins, outs = refs[: 2 * n], refs[2 * n :]
    for s in range(n):
        outs[s][...] = (ins[2 * s][...].astype(F32) + ins[2 * s + 1][...].astype(F32)).astype(BF16)


def pair_sum(me, which, mine, other, half, tile=512):
    n, width = which.shape[1], mine.shape[1]
    tile = fit(width, tile)
    picked = [pl.BlockSpec((half, tile), lambda i, me, w, s=s: (w[me[0] * n + s], i)) for s in range(n) for _ in range(2)]
    return call(
        functools.partial(pair_sum_kernel, n=n),
        (width // tile,),
        picked,
        [pl.BlockSpec((half, tile), lambda i, *_: (0, i))] * n,
        [jax.ShapeDtypeStruct((half, width), BF16)] * n,
        scalars=(me, which),
        vmem=SUM_VMEM,
        bytes_accessed=6 * n * half * width,
    )(me, jnp.asarray(which.reshape(-1), jnp.int32), *([mine, other] * n))


def place_kernel(me, _, valid, __, *refs, spans, total_slots):
    out, i = refs[-1], pl.program_id(0)
    flag = valid[me[0] * total_slots + i]
    at = 0
    for counts, n_picked in spans:
        picked = refs[at : at + n_picked]
        at += n_picked
        for slot, n_received in counts:
            mine = [*picked, *refs[at : at + n_received]]
            at += n_received

            @pl.when((flag == 1) & (i == slot))
            def _():
                total = mine[0][...].astype(F32)
                for r in mine[1:]:
                    total = total + r[...].astype(F32)
                out[...] = total.astype(BF16)

    if len(refs) > at + 1:

        @pl.when(flag == 2)
        def _():
            out[...] = refs[at][...]


def place(me, groups, out, shape, half):
    which = np.concatenate([g[0][0] for g in groups], axis=1)
    valid = np.concatenate([g[0][1] for g in groups], axis=1)
    where = np.concatenate([g[0][2] for g in groups], axis=1)
    n = which.shape[1]
    for d in range(len(valid)):
        real = np.flatnonzero(valid[d])
        if len(real) == 0:
            valid[d], where[d] = 2, 0
            continue
        for s in range(n):
            before = real[real <= s]
            near = before[-1] if len(before) else real[0]
            where[d, s] = where[d, near]
    width = shape[1]
    specs, args, spans, first = [], [], [], 0
    for tables, picked, received in groups:
        slots = tables[0].shape[1]
        at = lambda i, f=first, s=slots: jnp.clip(i, f, f + s - 1)
        specs += [pl.BlockSpec((half, width), lambda i, me, w, v, p, at=at: (w[me[0] * n + at(i)], 0)) for _ in picked]
        args += picked
        for r in received:
            specs += [pl.BlockSpec((half, width), lambda i, *_: (0, 0)) for _ in r]
            args += r
        spans.append(([(first + s, len(r)) for s, r in enumerate(received)], len(picked)))
        first += slots
    spec = pl.BlockSpec((half, width), lambda i, me, w, v, p: (p[me[0] * n + i], 0))
    aliases = {}
    kernel = functools.partial(place_kernel, spans=spans, total_slots=n)
    if out is not None:
        keep = (valid == 2).any()
        specs.append(spec if keep else pl.BlockSpec(memory_space=pl.ANY))
        args.append(out)
        aliases = {4 + len(args) - 1: 0}
        if not keep:
            inner = kernel
            kernel = lambda *refs: inner(*refs[:-2], refs[-1])
    return call(
        kernel,
        (n,),
        specs,
        spec,
        jax.ShapeDtypeStruct(shape, BF16),
        scalars=(me, which, valid, where),
        aliases=aliases,
        bytes_accessed=8 * n * half * width,
    )(me, *[jnp.asarray(t.reshape(-1), jnp.int32) for t in (which, valid, where)], *args)


def body(n_row, n_col, attn, grad_out, weight, momentum):
    ring = np.array(snake(n_row))
    pos = np.argsort(ring)
    right = [(int(ring[i]), int(ring[(i + 1) % n_row])) for i in range(n_row)]
    left = [(b, a) for a, b in right]
    block, cols = grad_out.shape
    half = block // 2
    per_owner = n_row // n_col
    n_y = n_col // 2
    devices = [(r, c) for r in range(n_row) for c in range(n_col)]
    me = (lax.axis_index("row") * n_col + lax.axis_index("col")).astype(jnp.int32).reshape(1)
    out_shape = (per_owner * block, weight.shape[0])

    arrives = np.zeros((n_row, n_row, 2), np.int32)
    for r in range(n_row):
        for k in range(n_row):
            arrives[r, k, 0] = 2 * ring[(pos[r] - k) % n_row]
            arrives[r, k, 1] = 2 * ring[(pos[r] + k) % n_row] + 1

    held = np.zeros((n_row * n_col, 2 * n_row), np.int32)
    for d, (r, c) in enumerate(devices):
        near = [(c + s) % n_col for s in range(0, n_col, 2)]
        for at, owner in enumerate(near + [o ^ 1 for o in near]):
            held[d, owner * 2 * per_owner : (owner + 1) * 2 * per_owner] = np.arange(2 * per_owner) + at * 2 * per_owner

    def order_of(steps):
        return np.stack([held[d, arrives[r, np.array(steps)].reshape(-1)] for d, (r, _) in enumerate(devices)])

    def tables_of(steps):
        halves = arrives[:, np.array(steps), :].reshape(n_row, -1)
        owner = halves // (2 * per_owner)
        slots = max(int(np.sum(owner[r] == c)) for r, c in devices)
        which, valid, where = (np.zeros((n_row * n_col, slots), np.int32) for _ in range(3))
        for d, (r, c) in enumerate(devices):
            own = np.flatnonzero(owner[r] == c)
            spots = list(halves[r, own] % (2 * per_owner))
            spots += [s for s in range(2 * per_owner) if s not in spots]
            which[d, : len(own)] = own
            valid[d, : len(own)] = 1
            where[d] = spots[:slots]
        return which, valid, where

    def route(valid, shift, slot):
        to = [(r, (c + shift) % n_col) for r, c in devices]
        return [(d, r * n_col + c) for d, (r, c) in enumerate(to) if valid[r * n_col + c, slot]]

    cores = [(c, c ^ 1) for c in range(n_col)]

    def send(arrays, valid, shift):
        return [lax.ppermute(x, ("row", "col"), route(valid, shift, s)) for s, x in enumerate(arrays)]

    def shifted(table, shift):
        return np.stack([table[r * n_col + (c + shift) % n_col] for r, c in devices])

    def reduce_in_pairs(steps, part, wait=0, hold=0, late=0):
        tables = tables_of(steps)
        for _ in range(wait):
            yield ()
        other = lax.ppermute(part, "col", cores)
        shifts = range(2, n_col, 2)
        sums = [pair_sum(me, shifted(tables[0], s), part, other, half) for s in shifts]
        for _ in range(1 + hold):
            other, sums = yield other, sums
        received = [send(sums[i], tables[1], s) for i, s in enumerate(shifts)]
        for _ in range(late):
            yield ()
        received = yield received
        done.append((tables, [part, other], [list(r) for r in zip(*received)]))

    def reduce_direct(step, parts):
        tables = tables_of([step])
        received = yield [send([parts[s]], tables[1], s)[0] for s in range(1, n_col)]
        done.append((tables, [], [[parts[0], *received]]))

    def sorted_part(step):
        which = tables_of([step])[0]
        take = np.concatenate([shifted(which, s) for s in range(n_col)], axis=1)
        return grad_in_part(pieces_of([step]), weight, take, me)

    arrived = {0: (grad_out[:half], grad_out[half:])}
    pieces_of = lambda steps: [(x,) for k in steps for x in arrived[k]]
    whole_pieces = lambda steps: [(x, 0) for k in steps for x in arrived[k]]

    top = n_row - 1
    mid = n_row // 2
    early = list(range(0, mid - 1))
    late = list(range(mid - 1, n_row))
    at_work = {
        1: ([0], 0, 2, 0),
        2: ([1], 2, 0, 0),
        mid - 1: (list(range(2, mid - 1)), 1, 0, 0),
        mid + 1: ([mid - 1, mid], 0, 0, 0),
        top - 1: (list(range(mid + 1, top - 1)), 0, 1, 0),
        top: ([top - 1], 0, 0, 0),
    }
    done, moving = [], []
    acc = grad_in = None

    def turn(on_link, work):
        nonlocal moving
        on_link, work, flights = tie(on_link, work, [f for _, f in moving])
        moving = [[g, f] for (g, _), f in zip(moving, flights)]
        return on_link, work

    def advance():
        nonlocal moving
        still = []
        for g, f in moving:
            try:
                still.append([g, g.send(f)])
            except StopIteration:
                pass
        moving = still

    def begin(g):
        moving.append([g, next(g)])

    for k in range(1, n_row):
        a, b = arrived[k - 1]
        nxt = (lax.ppermute(a, "row", right), lax.ppermute(b, "row", left))
        work = ()
        if k in at_work:
            work = grad_in_part(pieces_of(at_work[k][0]), weight)
        elif k == mid:
            work = token_pass(me, order_of(early), attn_all, whole_pieces(early), (momentum,), out_dtype=BF16, tile=1024)
        extra = ()
        if k == 1:
            far = [lax.ppermute(attn, "col", [(c, (c - s) % n_col) for c in range(n_col)]) for s in range(2, n_col, 2)]
            extra = lax.ppermute(attn, "col", cores)
        elif k == 2:
            extra = far
        elif k == 3:
            extra = jnp.concatenate([attn, *far, beside, *[lax.ppermute(x, "col", cores) for x in far]])
        elif k == top and done:
            extra = place(me, done, None, out_shape, half)
            done.clear()
        arrived[k], (work, extra) = turn(nxt, (work, extra))
        if k == 1:
            beside = extra
        elif k == 2:
            far = extra
        elif k == 3:
            attn_all = extra
        elif k == top and not isinstance(extra, tuple):
            grad_in = extra
        advance()
        if k in at_work:
            begin(reduce_in_pairs(at_work[k][0], work, *at_work[k][1:]))
        elif k == mid:
            acc = work
    parts = sorted_part(top)
    sums = [f for g, f in moving if len(f) == 2 and not isinstance(f, list)]
    parts, acc, sums = tie(parts, acc, sums)
    sums = iter(sums)
    moving = [[g, next(sums) if len(f) == 2 and not isinstance(f, list) else f] for g, f in moving]
    still = []
    for g, f in moving:
        still.append([g, g.send(f)] if not isinstance(f, list) else [g, f])
    moving = still
    begin(reduce_direct(top, parts))
    new_w, new_m = token_pass(me, order_of(late), attn_all, whole_pieces(late), (acc, weight))
    _, (new_w, new_m) = turn((), (new_w, new_m))
    while moving:
        advance()
    grad_in = place(me, done, grad_in, out_shape, half)
    return grad_in, new_w, new_m


def solution(mesh):
    n_row, n_col = mesh.shape["row"], mesh.shape["col"]
    spec, act = P("row", "col"), P("col", "row")

    def shards(attn, grad_out, weight, momentum):
        return body(n_row, n_col, attn, grad_out, weight, momentum)

    return jax.shard_map(shards, mesh=mesh, in_specs=(act, spec, spec, spec), out_specs=(act, spec, spec), check_vma=False)
```

```python
import functools

import jax
import jax.numpy as jnp
import numpy as np
from jax import lax
from jax.experimental import pallas as pl
from jax.experimental.pallas import tpu as pltpu
from jax.sharding import PartitionSpec as P

BF16 = jnp.bfloat16
F32 = jnp.float32
NT = (((1,), (1,)), ((), ()))
TN = (((0,), (0,)), ((), ()))
VMEM_BYTES = 60 << 20
GRAD_IN_VMEM, SUM_VMEM, LAST_VMEM = 50 << 20, 24 << 20, 46 << 20


def snake(n):
    return list(range(0, n, 2)) + list(range(n - 1 - (n % 2), 0, -2))


def tie(*xs):
    return lax.optimization_barrier(xs)


def fit(size, want):
    while size % want:
        want //= 2
    return want


def call(kernel, grid, in_specs, out_specs, out_shape, scalars=(), scratch=(), aliases=None, flops=0, bytes_accessed=0, vmem=VMEM_BYTES):
    return pl.pallas_call(
        kernel,
        grid_spec=pltpu.PrefetchScalarGridSpec(
            num_scalar_prefetch=len(scalars), grid=grid, in_specs=in_specs, out_specs=out_specs, scratch_shapes=scratch
        ),
        out_shape=out_shape,
        input_output_aliases=aliases or {},
        compiler_params=pltpu.CompilerParams(vmem_limit_bytes=vmem),
        cost_estimate=pl.CostEstimate(flops=flops, bytes_accessed=bytes_accessed, transcendentals=0),
    )


def tokens_of(refs, parts):
    halves = [refs[i : i + parts] for i in range(0, len(refs), parts)]
    rows = [h[0][...] if parts == 1 else jnp.concatenate([r[...] for r in h], axis=1) for h in halves]
    return jnp.concatenate(rows)


def grad_in_kernel(*refs, n, parts):
    total = lax.dot_general(tokens_of(refs[:n], parts), refs[n][...], NT, preferred_element_type=F32)
    refs[-1][...] = total.astype(BF16)


def grad_in_sorted_kernel(me, take, *refs, n, parts, n_out, half):
    total = lax.dot_general(tokens_of(refs[:n], parts), refs[n][...], NT, preferred_element_type=F32).astype(BF16)
    for s in range(n_out):
        upper = take[me[0] * n_out + s] > 0
        refs[n + 1 + s][...] = jnp.where(upper, total[half:], total[:half])


def grad_in_part(pieces, weight, take=None, me=None, tile=512):
    parts, half = len(pieces[0]), pieces[0][0].shape[0]
    feats, cols = weight.shape
    rows = half * len(pieces)
    tile = fit(feats, tile if rows > 2 * half else 2 * tile)
    flat = [x for p in pieces for x in p]
    specs = [pl.BlockSpec(x.shape, lambda i, *_: (0, 0)) for x in flat]
    specs.append(pl.BlockSpec((tile, cols), lambda i, *_: (i, 0)))
    cost = dict(vmem=GRAD_IN_VMEM, flops=2 * rows * feats * cols, bytes_accessed=2 * (rows * cols + feats * cols + rows * feats))
    if take is None:
        kernel = functools.partial(grad_in_kernel, n=len(flat), parts=parts)
        out = pl.BlockSpec((rows, tile), lambda i: (0, i))
        return call(kernel, (feats // tile,), specs, out, jax.ShapeDtypeStruct((rows, feats), BF16), **cost)(*flat, weight)
    n_out = take.shape[1]
    kernel = functools.partial(grad_in_sorted_kernel, n=len(flat), parts=parts, n_out=n_out, half=half)
    outs = [pl.BlockSpec((half, tile), lambda i, *_: (0, i))] * n_out
    shapes = [jax.ShapeDtypeStruct((half, feats), BF16)] * n_out
    return call(kernel, (feats // tile,), specs, outs, shapes, scalars=(me, take), **cost)(
        me, jnp.asarray(take.reshape(-1), jnp.int32), *flat, weight
    )


def assemble(dst, refs):
    at = 0
    for r in refs:
        dst[at : at + r.shape[0], :] = r[...]
        at += r.shape[0]


def pass_kernel(_, __, *refs, n, n_grads, last, n_old, rows):
    attn, grads, rest = refs[:n], refs[n : n + n_grads], refs[n + n_grads :]
    if last:
        acc_ref, w_ref = rest[:2]
        new_w, new_m, attn_s, grad_s = rest[2 + n_old :]
    else:
        m_ref, out, attn_s, grad_s = rest

    @pl.when(pl.program_id(0) == 0)
    def _():
        assemble(attn_s, attn)

    assemble(grad_s, grads)
    for c in range(0, attn_s.shape[1], rows):
        here = slice(c, c + rows)
        add = lax.dot_general(attn_s[:, here], grad_s[...], TN, preferred_element_type=F32)
        if last:
            mom = acc_ref[here].astype(F32) + add
            new_w[here] = (w_ref[here].astype(F32) - 0.25 * mom).astype(BF16)
            new_m[here] = mom.astype(BF16)
        else:
            out[here] = (0.9 * m_ref[here].astype(F32) + add).astype(out.dtype)


def token_pass(me, order, attn_all, pieces, wides, first_col=0, n_cols=None, old=(), out_dtype=None, tile=512):
    last = len(wides) == 2
    n = len(pieces)
    half = pieces[0][0].shape[0]
    feats, cols = wides[0].shape
    n_cols = n_cols or cols
    tile = fit(n_cols, tile)
    base = first_col // tile
    specs = [pl.BlockSpec((half, feats), lambda j, me, o, i=i: (o[me[0] * n + i], 0)) for i in range(n)]
    specs += [pl.BlockSpec((half, tile), lambda j, *_, c=(first_col - at) // tile: (0, j + c)) for _, at in pieces]
    wide = pl.BlockSpec((feats, tile), lambda j, *_: (0, j + base))
    specs += [wide] * len(wides) + [pl.BlockSpec(memory_space=pl.ANY)] * len(old)
    shape = jax.ShapeDtypeStruct((feats, cols), BF16 if last else out_dtype)
    return call(
        functools.partial(pass_kernel, n=n, n_grads=n, last=last, n_old=len(old), rows=fit(feats, 512)),
        (n_cols // tile,),
        specs,
        [wide, wide] if last else wide,
        [shape, shape] if last else shape,
        scalars=(me, order),
        scratch=[pltpu.VMEM((n * half, feats), BF16), pltpu.VMEM((n * half, tile), BF16)],
        aliases={2 + 2 * n + 2 + i: i for i in range(len(old))},
        vmem=LAST_VMEM,
        flops=2 * n * half * feats * n_cols,
        bytes_accessed=8 * feats * n_cols,
    )(me, jnp.asarray(order.reshape(-1), jnp.int32), *([attn_all] * n), *[x for x, _ in pieces], *wides, *old)


def pair_sum_kernel(_, __, *refs, n):
    ins, outs = refs[: 2 * n], refs[2 * n :]
    for s in range(n):
        outs[s][...] = (ins[2 * s][...].astype(F32) + ins[2 * s + 1][...].astype(F32)).astype(BF16)


def pair_sum(me, which, mine, other, half, tile=512):
    n, width = which.shape[1], mine.shape[1]
    tile = fit(width, tile)
    picked = [pl.BlockSpec((half, tile), lambda i, me, w, s=s: (w[me[0] * n + s], i)) for s in range(n) for _ in range(2)]
    return call(
        functools.partial(pair_sum_kernel, n=n),
        (width // tile,),
        picked,
        [pl.BlockSpec((half, tile), lambda i, *_: (0, i))] * n,
        [jax.ShapeDtypeStruct((half, width), BF16)] * n,
        scalars=(me, which),
        vmem=SUM_VMEM,
        bytes_accessed=6 * n * half * width,
    )(me, jnp.asarray(which.reshape(-1), jnp.int32), *([mine, other] * n))


def place_kernel(me, _, valid, __, *refs, spans, total_slots):
    out, i = refs[-1], pl.program_id(0)
    flag = valid[me[0] * total_slots + i]
    at = 0
    for counts, n_picked in spans:
        picked = refs[at : at + n_picked]
        at += n_picked
        for slot, n_received in counts:
            mine = [*picked, *refs[at : at + n_received]]
            at += n_received

            @pl.when((flag == 1) & (i == slot))
            def _():
                total = mine[0][...].astype(F32)
                for r in mine[1:]:
                    total = total + r[...].astype(F32)
                out[...] = total.astype(BF16)

    if len(refs) > at + 1:

        @pl.when(flag == 2)
        def _():
            out[...] = refs[at][...]


def place(me, groups, out, shape, half):
    which = np.concatenate([g[0][0] for g in groups], axis=1)
    valid = np.concatenate([g[0][1] for g in groups], axis=1)
    where = np.concatenate([g[0][2] for g in groups], axis=1)
    n = which.shape[1]
    for d in range(len(valid)):
        real = np.flatnonzero(valid[d])
        if len(real) == 0:
            valid[d], where[d] = 2, 0
            continue
        for s in range(n):
            before = real[real <= s]
            near = before[-1] if len(before) else real[0]
            where[d, s] = where[d, near]
    width = shape[1]
    specs, args, spans, first = [], [], [], 0
    for tables, picked, received in groups:
        slots = tables[0].shape[1]
        at = lambda i, f=first, s=slots: jnp.clip(i, f, f + s - 1)
        specs += [pl.BlockSpec((half, width), lambda i, me, w, v, p, at=at: (w[me[0] * n + at(i)], 0)) for _ in picked]
        args += picked
        for r in received:
            specs += [pl.BlockSpec((half, width), lambda i, *_: (0, 0)) for _ in r]
            args += r
        spans.append(([(first + s, len(r)) for s, r in enumerate(received)], len(picked)))
        first += slots
    spec = pl.BlockSpec((half, width), lambda i, me, w, v, p: (p[me[0] * n + i], 0))
    aliases = {}
    kernel = functools.partial(place_kernel, spans=spans, total_slots=n)
    if out is not None:
        keep = (valid == 2).any()
        specs.append(spec if keep else pl.BlockSpec(memory_space=pl.ANY))
        args.append(out)
        aliases = {4 + len(args) - 1: 0}
        if not keep:
            inner = kernel
            kernel = lambda *refs: inner(*refs[:-2], refs[-1])
    return call(
        kernel,
        (n,),
        specs,
        spec,
        jax.ShapeDtypeStruct(shape, BF16),
        scalars=(me, which, valid, where),
        aliases=aliases,
        bytes_accessed=8 * n * half * width,
    )(me, *[jnp.asarray(t.reshape(-1), jnp.int32) for t in (which, valid, where)], *args)


def body(n_row, n_col, attn, grad_out, weight, momentum):
    ring = np.array(snake(n_row))
    pos = np.argsort(ring)
    right = [(int(ring[i]), int(ring[(i + 1) % n_row])) for i in range(n_row)]
    left = [(b, a) for a, b in right]
    block, cols = grad_out.shape
    half = block // 2
    per_owner = n_row // n_col
    n_y = n_col // 2
    devices = [(r, c) for r in range(n_row) for c in range(n_col)]
    me = (lax.axis_index("row") * n_col + lax.axis_index("col")).astype(jnp.int32).reshape(1)
    out_shape = (per_owner * block, weight.shape[0])

    arrives = np.zeros((n_row, n_row, 2), np.int32)
    for r in range(n_row):
        for k in range(n_row):
            arrives[r, k, 0] = 2 * ring[(pos[r] - k) % n_row]
            arrives[r, k, 1] = 2 * ring[(pos[r] + k) % n_row] + 1

    held = np.zeros((n_row * n_col, 2 * n_row), np.int32)
    for d, (r, c) in enumerate(devices):
        near = [(c + s) % n_col for s in range(0, n_col, 2)]
        for at, owner in enumerate(near + [o ^ 1 for o in near]):
            held[d, owner * 2 * per_owner : (owner + 1) * 2 * per_owner] = np.arange(2 * per_owner) + at * 2 * per_owner

    def order_of(steps):
        return np.stack([held[d, arrives[r, np.array(steps)].reshape(-1)] for d, (r, _) in enumerate(devices)])

    def tables_of(steps):
        halves = arrives[:, np.array(steps), :].reshape(n_row, -1)
        owner = halves // (2 * per_owner)
        slots = max(int(np.sum(owner[r] == c)) for r, c in devices)
        which, valid, where = (np.zeros((n_row * n_col, slots), np.int32) for _ in range(3))
        for d, (r, c) in enumerate(devices):
            own = np.flatnonzero(owner[r] == c)
            spots = list(halves[r, own] % (2 * per_owner))
            spots += [s for s in range(2 * per_owner) if s not in spots]
            which[d, : len(own)] = own
            valid[d, : len(own)] = 1
            where[d] = spots[:slots]
        return which, valid, where

    def route(valid, shift, slot):
        to = [(r, (c + shift) % n_col) for r, c in devices]
        return [(d, r * n_col + c) for d, (r, c) in enumerate(to) if valid[r * n_col + c, slot]]

    cores = [(c, c ^ 1) for c in range(n_col)]

    def send(arrays, valid, shift):
        return [lax.ppermute(x, ("row", "col"), route(valid, shift, s)) for s, x in enumerate(arrays)]

    def shifted(table, shift):
        return np.stack([table[r * n_col + (c + shift) % n_col] for r, c in devices])

    def reduce_in_pairs(steps, part, wait=0, hold=0, late=0):
        tables = tables_of(steps)
        for _ in range(wait):
            yield ()
        other = lax.ppermute(part, "col", cores)
        shifts = range(2, n_col, 2)
        sums = [pair_sum(me, shifted(tables[0], s), part, other, half) for s in shifts]
        for _ in range(1 + hold):
            other, sums = yield other, sums
        received = [send(sums[i], tables[1], s) for i, s in enumerate(shifts)]
        for _ in range(late):
            yield ()
        received = yield received
        done.append((tables, [part, other], [list(r) for r in zip(*received)]))

    def reduce_direct(step, parts):
        tables = tables_of([step])
        received = yield [send([parts[s]], tables[1], s)[0] for s in range(1, n_col)]
        done.append((tables, [], [[parts[0], *received]]))

    def sorted_part(step):
        which = tables_of([step])[0]
        take = np.concatenate([shifted(which, s) for s in range(n_col)], axis=1)
        return grad_in_part(pieces_of([step]), weight, take, me)

    arrived = {0: (grad_out[:half], grad_out[half:])}
    pieces_of = lambda steps: [(x,) for k in steps for x in arrived[k]]
    whole_pieces = lambda steps: [(x, 0) for k in steps for x in arrived[k]]

    top = n_row - 1
    mid = n_row // 2
    early = list(range(0, mid - 1))
    late = list(range(mid - 1, n_row))
    at_work = {
        1: ([0], 0, 2, 0),
        2: ([1], 2, 0, 0),
        mid - 1: (list(range(2, mid - 1)), 1, 0, 0),
        mid + 1: ([mid - 1, mid], 0, 0, 0),
        top - 1: (list(range(mid + 1, top - 1)), 0, 1, 0),
        top: ([top - 1], 0, 0, 0),
    }
    done, moving = [], []
    acc = grad_in = None

    def turn(on_link, work):
        nonlocal moving
        on_link, work, flights = tie(on_link, work, [f for _, f in moving])
        moving = [[g, f] for (g, _), f in zip(moving, flights)]
        return on_link, work

    def advance():
        nonlocal moving
        still = []
        for g, f in moving:
            try:
                still.append([g, g.send(f)])
            except StopIteration:
                pass
        moving = still

    def begin(g):
        moving.append([g, next(g)])

    for k in range(1, n_row):
        a, b = arrived[k - 1]
        nxt = (lax.ppermute(a, "row", right), lax.ppermute(b, "row", left))
        work = ()
        if k in at_work:
            work = grad_in_part(pieces_of(at_work[k][0]), weight)
        elif k == mid:
            work = token_pass(me, order_of(early), attn_all, whole_pieces(early), (momentum,), out_dtype=BF16, tile=1024)
        extra = ()
        if k == 1:
            far = [lax.ppermute(attn, "col", [(c, (c - s) % n_col) for c in range(n_col)]) for s in range(2, n_col, 2)]
            extra = lax.ppermute(attn, "col", cores)
        elif k == 2:
            extra = far
        elif k == 3:
            extra = jnp.concatenate([attn, *far, beside, *[lax.ppermute(x, "col", cores) for x in far]])
        elif k == top and done:
            extra = place(me, done, None, out_shape, half)
            done.clear()
        arrived[k], (work, extra) = turn(nxt, (work, extra))
        if k == 1:
            beside = extra
        elif k == 2:
            far = extra
        elif k == 3:
            attn_all = extra
        elif k == top and not isinstance(extra, tuple):
            grad_in = extra
        advance()
        if k in at_work:
            begin(reduce_in_pairs(at_work[k][0], work, *at_work[k][1:]))
        elif k == mid:
            acc = work
    parts = sorted_part(top)
    sums = [f for g, f in moving if len(f) == 2 and not isinstance(f, list)]
    parts, acc, sums = tie(parts, acc, sums)
    sums = iter(sums)
    moving = [[g, next(sums) if len(f) == 2 and not isinstance(f, list) else f] for g, f in moving]
    still = []
    for g, f in moving:
        still.append([g, g.send(f)] if not isinstance(f, list) else [g, f])
    moving = still
    begin(reduce_direct(top, parts))
    new_w, new_m = token_pass(me, order_of(late), attn_all, whole_pieces(late), (acc, weight))
    _, (new_w, new_m) = turn((), (new_w, new_m))
    while moving:
        advance()
    grad_in = place(me, done, grad_in, out_shape, half)
    return grad_in, new_w, new_m


def solution(mesh):
    n_row, n_col = mesh.shape["row"], mesh.shape["col"]
    spec, act = P("row", "col"), P("col", "row")

    def shards(attn, grad_out, weight, momentum):
        return body(n_row, n_col, attn, grad_out, weight, momentum)

    return jax.shard_map(shards, mesh=mesh, in_specs=(act, spec, spec, spec), out_specs=(act, spec, spec), check_vma=False)
```
